256 devices in a mesh: dp: 32 (over z, y), tensor: 8 (over x, core).
Axes of the slice: x: 4, y: 4, z: 8, core: 2. Of those that a mesh axis runs over, the one named last changes fastest.
Arguments:
- inputs: bfloat16 [2, 4096, 4096], P(None, 'dp', 'tensor'), may hold values from -6 to 6
- out_grads: bfloat16 [2, 4096, 4096], P(None, 'dp', 'tensor'), may hold values from -6 to 6
- momentum: bfloat16 [32, 4096, 4096], P('dp', None, 'tensor'), may hold values from -6 to 6
- band: int32 [64, 64, 2, 8], P(None, 'tensor'), may hold values from 0 to 15, as said below
Outputs:
- new_momentum: bfloat16 [32, 4096, 4096], P('dp', None, 'tensor')
- update: float32 [4096, 4096], P('dp', 'tensor')
The draws below stay inside these ranges and needn't reach their ends.
Inputs may be any that keep to these rules, and one draw needn't show every extreme that they name: Each band[r, c, s, :] holds 8 different frequencies of 0 to 15 in rising order.
All inputs are finite; a program needn't handle non-finite values.
Results may differ from the reference program's by a relative error of at most 0.001.
Values may be sent and summed in bfloat16 or wider, within the bound.
A program may use at most 128 MiB of HBM per device.

```python
import math
import jax
import jax.numpy as jnp
from jax import lax

D_IN = 4096
D_OUT = 4096
SPAN = 64
BAND = 8
LOW = 16
STEPS = 2
TOK_DEV = 128
TOKENS = 4096
REPLICAS = 32
SPAN_ROWS = 64
SPAN_COLS = 64


def draw_band(key, part):
    key = jax.random.fold_in(key, 11)
    scores = jax.random.randint(key, (SPAN_ROWS, SPAN_COLS, 2, LOW), 0, 1 << 20, dtype=jnp.int32)
    scores = scores * LOW + jnp.arange(LOW, dtype=jnp.int32)
    order = jnp.argsort(scores, axis=-1).astype(jnp.int32)
    return jnp.sort(order[..., :BAND], axis=-1).astype(jnp.int32)


def level_of(stream_key, shape, split, smallest, top_value):
    loudness, own = 1.0, jax.random.fold_in(stream_key, 6)
    for axis_at, shards_of in split:
        draws = jnp.exp(jax.random.uniform(jax.random.fold_in(own, axis_at), (shards_of,), jnp.float32, smallest / len(split), top_value / len(split)))
        loudness = loudness * jnp.repeat(draws, shape[axis_at] // shards_of).reshape([-1 if axis == axis_at else 1 for axis in range(len(shape))])
    return loudness


def bell_draw(stream_key, dims, deviation, limit, cuts=(), kind=jnp.bfloat16):
    values = deviation * jax.random.normal(stream_key, dims, jnp.float32)
    if cuts:
        values = values * level_of(stream_key, dims, cuts, -0.22, 0.18)
    return jnp.clip(values, -limit, limit).astype(kind)


def setup_inputs(seed: int = 0) -> dict:
    streams_of = jax.random.split(jax.random.key(seed), 5)
    inputs = bell_draw(streams_of[0], (STEPS, TOKENS, D_IN), 1.0, 6.0, ((1, 32), (2, 8)))
    out_grads = bell_draw(streams_of[1], (STEPS, TOKENS, D_OUT), 1.0, 6.0, ((1, 32), (2, 8)))
    momentum = bell_draw(streams_of[2], (REPLICAS, D_IN, D_OUT), 1.0, 6.0, ((0, 32), (2, 8)))
    band = draw_band(jax.random.fold_in(streams_of[4], 71), 0)
    return {"inputs": inputs, "out_grads": out_grads, "momentum": momentum, "band": band}


def dct_basis():
    freq = jnp.arange(SPAN, dtype=jnp.float32)[:, None]
    place = jnp.arange(SPAN, dtype=jnp.float32)[None, :]
    table = jnp.sqrt(2.0 / SPAN) * jnp.cos(math.pi * (2.0 * place + 1.0) * freq / (2.0 * SPAN))
    first = jnp.where(jnp.arange(SPAN)[:, None] == 0, 1.0 / math.sqrt(2.0), 1.0)
    return (table * first).astype(jnp.float32)

def reference(inputs, out_grads, momentum, band):
    basis = dct_basis()
    picked = basis[band]
    rows_pick = picked[:, :, 0]
    cols_pick = picked[:, :, 1]
    factor = 1.0 / math.sqrt(TOK_DEV)

    def replica(total, index):
        start = index * TOK_DEV
        state = momentum[index].astype(jnp.float32)
        for step in range(STEPS):
            left = lax.dynamic_slice_in_dim(inputs[step], start, TOK_DEV, 0)
            right = lax.dynamic_slice_in_dim(out_grads[step], start, TOK_DEV, 0)
            grad = jnp.dot(left.T, right, preferred_element_type=jnp.float32) * factor
            state = 0.9 * state + grad
            blocks = state.reshape(SPAN_ROWS, SPAN, SPAN_COLS, SPAN)
            half = jnp.einsum('rcai,ricj->rcaj', rows_pick, blocks, precision=lax.Precision.HIGHEST)
            coeffs = jnp.einsum('rcaj,rcbj->rcab', half, cols_pick, precision=lax.Precision.HIGHEST)
            back = jnp.einsum('rcai,rcab->rcib', rows_pick, coeffs, precision=lax.Precision.HIGHEST)
            loss = jnp.einsum('rcib,rcbj->ricj', back, cols_pick, precision=lax.Precision.HIGHEST)
            state = (blocks - loss).reshape(D_IN, D_OUT)
            total = total + coeffs
        return (total, state.astype(jnp.bfloat16))
    start_total = jnp.zeros((SPAN_ROWS, SPAN_COLS, BAND, BAND), jnp.float32)
    total, new_momentum = lax.scan(replica, start_total, jnp.arange(REPLICAS, dtype=jnp.int32))
    back = jnp.einsum('rcai,rcab->rcib', rows_pick, total, precision=lax.Precision.HIGHEST)
    update = jnp.einsum('rcib,rcbj->ricj', back, cols_pick, precision=lax.Precision.HIGHEST)
    return (new_momentum, update.reshape(D_IN, D_OUT))
```

```python
import functools
import math

import jax
import jax.numpy as jnp
import numpy as np
from jax import lax
from jax.experimental import pallas as pl
from jax.experimental.pallas import tpu as pltpu
from jax.sharding import PartitionSpec as P

MESH = pl.DeviceIdType.MESH
F32 = jnp.float32
BF16 = jnp.bfloat16
SPAN = 64
LOW = 16
BAND = 8
TOK = 128
ROWS = 4096
COLS = 512
SHARD = 512
STEPS = 2
X = 4
GROUPS = 32
Y = 4
PIECES = 4
PIECE = SHARD // PIECES
CHUNKS = 8
FACTOR = 1.0 / math.sqrt(TOK)


def low_rows():
    freq = np.arange(LOW)[:, None]
    place = np.arange(SPAN)[None, :]
    table = np.sqrt(2.0 / SPAN) * np.cos(math.pi * (2.0 * place + 1.0) * freq / (2.0 * SPAN))
    table[0] /= math.sqrt(2.0)
    return table.astype(np.float32)


def constants():
    low = low_rows()
    enc = np.zeros((LOW, 8, 8, SPAN), np.float32)
    col = np.zeros((8, SPAN, 8, LOW), np.float32)
    for block in range(8):
        enc[:, block, block, :] = low
        col[block, :, block, :] = low.T
    enc = enc.reshape(128, 512)
    col = col.reshape(512, 128)
    return np.concatenate([enc, col.T], axis=0), np.concatenate([enc.T, col], axis=1)


def split(a):
    high = a.astype(BF16)
    low = (a - high.astype(F32)).astype(BF16)
    return high, low


def mm(a, b):
    return jnp.dot(a, b, preferred_element_type=F32)


def kernel(
    x_hbm, d_hbm, m_hbm, band_hbm, flat_hbm, tall_hbm,
    out_ref, upd_ref,
    xin, din, m_ref, band_ref, flat, upright, rowenc, rowdec, colenc, coldec,
    xt, val, colmask, wx, rhs, gm, send, recv, tot,
    load_sem, m_sem, gather_send, gather_recv, sum_send, sum_recv,
):
    dp = lax.axis_index("dp")
    tensor = lax.axis_index("tensor")
    cx = tensor // 2
    core = tensor % 2
    cz = dp // Y
    cy = dp % Y

    def tensor_of(step, other):
        return 2 * ((cx + step) % X) + (core + other) % 2

    mate = tensor_of(0, 1)
    right = tensor_of(1, 0)
    left = tensor_of(X - 1, 0)

    barrier = pltpu.get_barrier_semaphore()
    for peer in (mate, right, left):
        pl.semaphore_signal(barrier, inc=1, device_id=(dp, peer), device_id_type=MESH)

    def greet(i, carry):
        pl.semaphore_signal(
            barrier, inc=1, device_id=((dp + i) % GROUPS, tensor), device_id_type=MESH
        )
        return carry

    lax.fori_loop(1, GROUPS, greet, 0)

    loads = []
    for n, (src, dst) in enumerate(
        [(x_hbm, xin), (tall_hbm, upright), (flat_hbm, flat), (d_hbm, din), (band_hbm, band_ref)]
    ):
        copy = pltpu.make_async_copy(src, dst, load_sem.at[n])
        copy.start()
        loads.append(copy)
    x_load, tall_load, flat_load, d_load, band_load = loads

    def m_copy(q):
        rows = pl.ds(pl.multiple_of(q * SHARD, SHARD), SHARD)
        return pltpu.make_async_copy(m_hbm.at[0, rows, :], m_ref.at[rows, :], m_sem.at[q])

    def start_m(q, carry):
        m_copy(q).start()
        return carry

    lax.fori_loop(0, CHUNKS, start_m, 0)

    own = pl.multiple_of(tensor * SHARD, SHARD)
    x_load.wait()
    for step in range(STEPS):
        xt[pl.ds(own, SHARD), step * TOK:(step + 1) * TOK] = xin[step].T

    pl.semaphore_wait(barrier, 3 + GROUPS - 1)

    def piece_copy(owner, piece, target):
        rows = pl.ds(pl.multiple_of(owner * SHARD + piece * PIECE, PIECE), PIECE)
        return pltpu.make_async_remote_copy(
            src_ref=xt.at[rows, :],
            dst_ref=xt.at[rows, :],
            send_sem=gather_send,
            recv_sem=gather_recv.at[owner * PIECES + piece],
            device_id=(dp, target),
            device_id_type=MESH,
        )

    for piece in range(PIECES):
        flip = (piece + PIECES // 2) % PIECES
        piece_copy(tensor, piece, right).start()
        piece_copy(tensor, flip, left).start()
    for piece in range(PIECES):
        piece_copy(tensor, piece, mate).start()

    tall_load.wait()
    flat_load.wait()
    high, low = split(upright[...])
    rowdec[:, 0:128] = high[:, 0:128]
    rowdec[:, 128:256] = low[:, 0:128]
    colenc[:, 0:128] = high[:, 128:256]
    colenc[:, 128:256] = low[:, 128:256]
    high, low = split(flat[...])
    rowenc[0:128, :] = high[0:128]
    rowenc[128:256, :] = low[0:128]
    coldec[0:128, :] = high[128:256]
    coldec[128:256, :] = high[128:256]
    coldec[256:384, :] = low[128:256]
    d_load.wait()
    hats = []
    for step in range(STEPS):
        both = mm(din[step], colenc[...])
        hats.append((both[:, :128] + both[:, 128:]) * FACTOR)
    table = jnp.concatenate(
        [jnp.concatenate([0.9 * hats[0], hats[0]], axis=1), jnp.concatenate([hats[1], hats[1]], axis=1)], axis=0
    )
    high, low = split(table)
    wx[0:256, :] = high
    wx[256:512, :] = high
    wx[512:768, :] = low
    high, low = split(0.9 * din[0].astype(F32))
    rhs[0:128, :] = high
    rhs[128:256, :] = din[1]
    rhs[256:384, :] = low

    band_load.wait()
    picks = band_ref[...].reshape(128, 64).astype(F32).T.astype(BF16)
    away = lax.broadcasted_iota(jnp.int32, (128, 128), 0) - lax.broadcasted_iota(jnp.int32, (128, 128), 1) // LOW * 16
    for n in range(2 * BAND):
        val[:, n * 128:(n + 1) * 128] = mm(picks, (away == n).astype(F32).astype(BF16))
    place = (lax.broadcasted_iota(jnp.int32, (64, 128), 1) % LOW).astype(F32)
    seen = jnp.zeros((64, 128), F32)
    for k in range(BAND):
        seen = jnp.where(val[:, (BAND + k) * 128:(BAND + k + 1) * 128] == place, 1.0, seen)
    colmask[...] = seen

    def momentum_part(q):
        m_copy(q).wait()
        rows = pl.ds(pl.multiple_of(q * SHARD, SHARD), SHARD)
        tall = mm(rowenc[...], m_ref[rows, :])
        high, low = split(tall[:128] + tall[128:])
        both = mm(jnp.concatenate([high, low], axis=0), colenc[...])
        gm[pl.ds(pl.multiple_of(q * 128, 128), 128), :] = both[:128, :128] + both[128:, :128] + both[:128, 128:]

    def momentum_step(q, carry):
        momentum_part(q)
        return carry

    lax.fori_loop(0, CHUNKS // 2, momentum_step, 0)
    half = PIECES // 2
    for piece in range(half):
        piece_copy(left, piece, right).wait_recv()
        piece_copy(left, piece, right).start()
        piece_copy(right, piece + half, left).wait_recv()
        piece_copy(right, piece + half, left).start()
    for piece in range(half):
        piece_copy(left, piece, mate).start()
        piece_copy(right, piece + half, mate).start()
    lax.fori_loop(CHUNKS // 2, CHUNKS, momentum_step, 0)

    def sum_copy(q, i):
        return pltpu.make_async_remote_copy(
            src_ref=send.at[q, pl.ds(i * 16, 16), :],
            dst_ref=recv.at[dp],
            send_sem=sum_send,
            recv_sem=sum_recv,
            device_id=(q * Y + i, tensor),
            device_id_type=MESH,
        )

    def shard_step(s, carry):
        pair = s // 2
        hop = jnp.where(pair == 1, X - 1, jnp.where(pair == 2, 1, jnp.where(pair == 3, 2, 0)))
        q = tensor_of(hop, s % 2)

        @pl.when(s == 2)
        def _():
            for piece in range(half):
                piece_copy(left, piece + half, mate).wait_recv()
                piece_copy(left, piece + half, mate).start()
                piece_copy(right, piece, mate).wait_recv()
                piece_copy(right, piece, mate).start()

        @pl.when(s == 6)
        def _():
            for piece in range(PIECES):
                piece_copy(q, piece, mate).wait_recv()
                piece_copy(q, piece, mate).start()

        @pl.when(s % 2 == 1)
        def _():
            for piece in range(PIECES):
                piece_copy(q, piece, mate).wait_recv()

        rows = pl.ds(pl.multiple_of(q * SHARD, SHARD), SHARD)
        tall = mm(rowenc[...], xt[rows, :])
        high, low = split(tall[:128] + tall[128:])
        grid = mm(jnp.concatenate([high, low, high], axis=1), wx[...])
        base = gm[pl.ds(pl.multiple_of(q * 128, 128), 128), :]
        grid_a = grid[:, :128] + 0.81 * base
        grid_b = grid[:, 128:] + 0.9 * base

        eight = pl.ds(pl.multiple_of(q * 8, 8), 8)
        mask = colmask[eight, :]
        vals = [val[eight, k * 128:(k + 1) * 128] for k in range(BAND)]
        for k in range(BAND):
            got = grid_b[8 * k:8 * k + 8]
            for f in range(k + 1, k + 9):
                got = jnp.where(vals[k] == f, grid_b[8 * f:8 * f + 8], got)
            send[q, pl.ds(k, 8, stride=8), :] = got * mask
        for i in range(Y):
            @pl.when(q * Y + i != dp)
            def _():
                sum_copy(q, i).start()

        kept = []
        for f in range(LOW):
            hit = jnp.zeros((8, 128), F32)
            for k in range(max(0, f - 8), min(7, f) + 1):
                hit = jnp.where(vals[k] == f, mask, hit)
            kept.append(hit * grid_a[8 * f:8 * f + 8])
        high, low = split(jnp.concatenate(kept, axis=0))
        wide = mm(jnp.concatenate([high, low, high], axis=1), coldec[...]) * (-1.0 / FACTOR)
        high, low = split(wide)
        rhs[384:512, :] = high
        rhs[512:640, :] = low
        rhs[640:768, :] = high
        for part in range(2):
            here = pl.ds(pl.multiple_of(q * SHARD + part * 256, 256), 256)
            feats = xt[here, :]
            dec = rowdec[part * 256:(part + 1) * 256, :]
            left_side = jnp.concatenate([feats, feats[:, :128], dec[:, :128], dec], axis=1)
            change = mm(left_side, rhs[...])
            out_ref[0, here, :] = (0.81 * m_ref[here, :].astype(F32) + FACTOR * change).astype(BF16)
        return carry

    lax.fori_loop(0, CHUNKS, shard_step, 0)

    everyone = recv.at[pl.ds(0, GROUPS - 1)]
    pltpu.make_async_copy(everyone, everyone, sum_recv).wait()
    total = send[cz, pl.ds(pl.multiple_of(cy * 16, 16), 16), :]
    recv[dp] = total
    total = jnp.sum(recv[...], axis=0)
    tot[...] = jnp.zeros((64, 128), F32)
    tot[pl.ds(pl.multiple_of(cy * 16, 16), 16), :] = total
    eight = pl.ds(pl.multiple_of(cz * 8, 8), 8)
    vals = [val[eight, k * 128:(k + 1) * 128] for k in range(BAND)]
    sums = [tot[pl.ds(k, 8, stride=8), :] for k in range(BAND)]
    kept = []
    for f in range(LOW):
        hit = jnp.zeros((8, 128), F32)
        for k in range(max(0, f - 8), min(7, f) + 1):
            hit = jnp.where(vals[k] == f, sums[k], hit)
        kept.append(hit)
    high, low = split(jnp.concatenate(kept, axis=0))
    wide = mm(jnp.concatenate([high, low, high], axis=1), coldec[...])
    high, low = split(wide)
    dec = rowdec[pl.ds(pl.multiple_of(cy * 128, 128), 128), :]
    upd_ref[...] = mm(
        jnp.concatenate([dec[:, :128], dec], axis=1), jnp.concatenate([high, low, high], axis=0)
    )

    everyone_sent = recv.at[pl.ds(0, GROUPS - 1)]
    pltpu.make_async_copy(everyone_sent, everyone_sent, sum_send).wait()
    sent = xt.at[pl.ds(0, 7 * SHARD), :]
    pltpu.make_async_copy(sent, sent, gather_send).wait()


def shards(inputs, out_grads, momentum, band):
    consts = [jnp.asarray(c) for c in constants()]
    band_t = jnp.transpose(band, (1, 2, 3, 0))
    hbm = pl.BlockSpec(memory_space=pltpu.HBM)
    vmem = pl.BlockSpec(memory_space=pltpu.VMEM)
    return pl.pallas_call(
        kernel,
        out_shape=(
            jax.ShapeDtypeStruct(momentum.shape, BF16),
            jax.ShapeDtypeStruct((128, COLS), F32),
        ),
        in_specs=[hbm] * 6,
        out_specs=(vmem, vmem),
        scratch_shapes=[
            pltpu.VMEM((STEPS, TOK, SHARD), BF16),
            pltpu.VMEM((STEPS, TOK, COLS), BF16),
            pltpu.VMEM((ROWS, COLS), BF16),
            pltpu.VMEM((8, 2, 8, 64), jnp.int32),
            pltpu.VMEM((256, 512), F32),
            pltpu.VMEM((512, 256), F32),
            pltpu.VMEM((256, 512), BF16),
            pltpu.VMEM((512, 256), BF16),
            pltpu.VMEM((512, 256), BF16),
            pltpu.VMEM((384, 512), BF16),
            pltpu.VMEM((ROWS, STEPS * TOK), BF16),
            pltpu.VMEM((64, 2048), F32),
            pltpu.VMEM((64, 128), F32),
            pltpu.VMEM((768, 256), BF16),
            pltpu.VMEM((768, COLS), BF16),
            pltpu.VMEM((1024, 128), F32),
            pltpu.VMEM((CHUNKS, 64, 128), F32),
            pltpu.VMEM((GROUPS, 16, 128), F32),
            pltpu.VMEM((64, 128), F32),
            pltpu.SemaphoreType.DMA((5,)),
            pltpu.SemaphoreType.DMA((CHUNKS,)),
            pltpu.SemaphoreType.DMA,
            pltpu.SemaphoreType.DMA((CHUNKS * PIECES,)),
            pltpu.SemaphoreType.DMA,
            pltpu.SemaphoreType.DMA,
        ],
        compiler_params=pltpu.CompilerParams(
            collective_id=0, has_side_effects=True, vmem_limit_bytes=40 * 1024 * 1024
        ),
        name="demo_steps",
    )(inputs, out_grads, momentum, band_t, *consts)


def solution(mesh):
    return jax.shard_map(
        shards,
        mesh=mesh,
        in_specs=(
            P(None, "dp", "tensor"),
            P(None, "dp", "tensor"),
            P("dp", None, "tensor"),
            P(None, "tensor", None, None),
        ),
        out_specs=(P("dp", None, "tensor"), P("dp", "tensor")),
        check_vma=False,
    )
```

```python
import functools
import math

import jax
import jax.numpy as jnp
import numpy as np
from jax import lax
from jax.experimental import pallas as pl
from jax.experimental.pallas import tpu as pltpu
from jax.sharding import PartitionSpec as P

MESH = pl.DeviceIdType.MESH
F32 = jnp.float32
BF16 = jnp.bfloat16
SPAN = 64
LOW = 16
BAND = 8
TOK = 128
ROWS = 4096
COLS = 512
SHARD = 512
STEPS = 2
X = 4
GROUPS = 32
Y = 4
HALF = SHARD // 2
CHUNKS = 8
FACTOR = 1.0 / math.sqrt(TOK)


def low_rows():
    freq = np.arange(LOW)[:, None]
    place = np.arange(SPAN)[None, :]
    table = np.sqrt(2.0 / SPAN) * np.cos(math.pi * (2.0 * place + 1.0) * freq / (2.0 * SPAN))
    table[0] /= math.sqrt(2.0)
    return table.astype(np.float32)


def constants():
    low = low_rows()
    enc = np.zeros((LOW, 8, 8, SPAN), np.float32)
    col = np.zeros((8, SPAN, 8, LOW), np.float32)
    for block in range(8):
        enc[:, block, block, :] = low
        col[block, :, block, :] = low.T
    enc = enc.reshape(128, 512)
    col = col.reshape(512, 128)
    return np.concatenate([enc, col.T], axis=0), np.concatenate([enc.T, col], axis=1)


def split(a):
    high = a.astype(BF16)
    low = (a - high.astype(F32)).astype(BF16)
    return high, low


def mm(a, b):
    return jnp.dot(a, b, preferred_element_type=F32)


def kernel(
    x_hbm, d_hbm, m_hbm, band_hbm, flat_hbm, tall_hbm,
    out_ref, upd_ref,
    xin, din, m_ref, band_ref, flat, upright, rowenc, rowdec, colenc, coldec,
    xt, val, colmask, pull, push, wx, rhs, gm, send, recv, tot,
    load_sem, m_sem, gather_send, gather_recv, sum_send, sum_recv,
):
    dp = lax.axis_index("dp")
    tensor = lax.axis_index("tensor")
    cx = tensor // 2
    core = tensor % 2
    cz = dp // Y
    cy = dp % Y

    def tensor_of(hop, other):
        return 2 * ((cx + hop) % X) + (core + other) % 2

    mate = tensor_of(0, 1)
    right = tensor_of(1, 0)
    left = tensor_of(X - 1, 0)
    opposite = tensor_of(2, 0)

    def load(src, dst, n):
        copy = pltpu.make_async_copy(src, dst, load_sem.at[n])
        copy.start()
        return copy

    x_loads = [
        load(x_hbm.at[:, :, half * 256:(half + 1) * 256], xin.at[:, :, half * 256:(half + 1) * 256], half)
        for half in range(2)
    ]
    barrier = pltpu.get_barrier_semaphore()
    for peer in (mate, right, left):
        pl.semaphore_signal(barrier, inc=1, device_id=(dp, peer), device_id_type=MESH)
    tall_load = load(tall_hbm, upright, 2)
    flat_load = load(flat_hbm, flat, 3)
    d_load = load(d_hbm, din, 4)
    band_load = load(band_hbm, band_ref, 5)

    def m_copy(p):
        rows = pl.ds(pl.multiple_of(p * 2 * SHARD, 2 * SHARD), 2 * SHARD)
        return pltpu.make_async_copy(m_hbm.at[0, rows, :], m_ref.at[rows, :], m_sem.at[p])

    for p in range(X):
        m_copy(p).start()

    def greet(i, carry):
        pl.semaphore_signal(
            barrier, inc=1, device_id=((dp + i) % GROUPS, tensor), device_id_type=MESH
        )
        return carry

    lax.fori_loop(1, GROUPS, greet, 0)

    def half_copy(owner, half, target):
        rows = pl.ds(pl.multiple_of(owner * SHARD + half * HALF, HALF), HALF)
        return pltpu.make_async_remote_copy(
            src_ref=xt.at[rows, :],
            dst_ref=xt.at[rows, :],
            send_sem=gather_send,
            recv_sem=gather_recv.at[owner * 2 + half],
            device_id=(dp, target),
            device_id_type=MESH,
        )

    def turn(half):
        x_loads[half].wait()
        rows = pl.ds(pl.multiple_of(tensor * SHARD + half * HALF, HALF), HALF)
        for step in range(STEPS):
            xt[rows, step * TOK:(step + 1) * TOK] = xin[step, :, half * HALF:(half + 1) * HALF].T

    turn(0)
    pl.semaphore_wait(barrier, 3 + GROUPS - 1)
    half_copy(tensor, 0, right).start()
    turn(1)
    half_copy(tensor, 1, left).start()
    half_copy(tensor, 0, mate).start()
    half_copy(tensor, 1, mate).start()
    half_copy(tensor, 1, right).start()
    half_copy(tensor, 0, left).start()

    tall_load.wait()
    flat_load.wait()
    high, low = split(upright[...])
    rowdec[:, 0:128] = high[:, 0:128]
    rowdec[:, 128:256] = low[:, 0:128]
    colenc[:, 0:128] = high[:, 128:256]
    colenc[:, 128:256] = low[:, 128:256]
    high, low = split(flat[...])
    rowenc[0:128, :] = high[0:128]
    rowenc[128:256, :] = low[0:128]
    coldec[0:128, :] = high[128:256]
    coldec[128:256, :] = high[128:256]
    coldec[256:384, :] = low[128:256]
    d_load.wait()
    both = mm(jnp.concatenate([din[0], din[1]], axis=0), colenc[...])
    hats = (both[:, :128] + both[:, 128:]) * FACTOR
    table = jnp.concatenate(
        [jnp.concatenate([0.9 * hats[:128], hats[:128]], axis=1), jnp.concatenate([hats[128:], hats[128:]], axis=1)],
        axis=0,
    )
    high, low = split(table)
    wx[0:256, :] = high
    wx[256:512, :] = high
    wx[512:768, :] = low
    high, low = split(0.9 * din[0].astype(F32))
    for unit in range(2):
        rhs[unit, 0:128, :] = high
        rhs[unit, 128:256, :] = din[1]
        rhs[unit, 256:384, :] = low

    band_load.wait()
    picks = band_ref[...].reshape(128, 64).astype(F32).T.astype(BF16)
    away = lax.broadcasted_iota(jnp.int32, (128, 128), 0) - lax.broadcasted_iota(jnp.int32, (128, 128), 1) // LOW * 16
    for n in range(2 * BAND):
        val[:, n * 128:(n + 1) * 128] = mm(picks, (away == n).astype(F32).astype(BF16))
    place = (lax.broadcasted_iota(jnp.int32, (64, 128), 1) % LOW).astype(F32)
    seen = jnp.zeros((64, 128), F32)
    ahead = jnp.zeros((64, 128), F32)
    back = jnp.full((64, 128), -1.0, F32)
    for k in range(BAND):
        freq = val[:, (BAND + k) * 128:(BAND + k + 1) * 128]
        seen = jnp.where(freq == place, 1.0, seen)
        back = jnp.where(freq == place, place - k, back)
        ahead = jnp.where(place == k, freq - k, ahead)
    colmask[...] = seen
    pull[...] = ahead
    push[...] = back

    def momentum_step(p, carry):
        m_copy(p).wait()
        rows = pl.ds(pl.multiple_of(p * 2 * SHARD, 2 * SHARD), 2 * SHARD)
        thin = mm(m_ref[rows, :], colenc[...])
        high, low = split(thin[:, :128] + thin[:, 128:])
        both = mm(
            rowenc[...], jnp.concatenate([high[:SHARD], low[:SHARD], high[SHARD:], low[SHARD:]], axis=1)
        )
        for unit in range(2):
            at = unit * 256
            gm[2 * p + unit] = both[:128, at:at + 128] + both[:128, at + 128:at + 256] + both[128:, at:at + 128]
        return carry

    lax.fori_loop(0, X, momentum_step, 0)

    top = lax.broadcasted_iota(jnp.int32, (8, 128), 0) < 4
    lane = lax.broadcasted_iota(jnp.int32, (8, 128), 1) % LOW < BAND

    def eight_of(ref, owner):
        return ref[pl.ds(pl.multiple_of(owner * 8, 8), 8), :]

    def pair_step(s, carry):
        hop_a = jnp.where(s == 0, 0, jnp.where(s == 1, X - 1, jnp.where(s == 2, 1, 2)))
        hop_b = jnp.where(s == 0, 0, jnp.where(s == 1, 1, jnp.where(s == 2, X - 1, 2)))
        owners = [(tensor_of(hop_a, other), tensor_of(hop_b, other)) for other in range(2)]

        @pl.when(s > 0)
        def _():
            half_copy(owners[0][0], 0, mate).wait_recv()
            half_copy(owners[0][0], 0, mate).start()

            @pl.when(s == 1)
            def _():
                half_copy(left, 0, right).start()

            half_copy(owners[0][1], 1, mate).wait_recv()
            half_copy(owners[0][1], 1, mate).start()

            @pl.when(s == 1)
            def _():
                half_copy(right, 1, left).start()

        half_copy(owners[1][0], 0, mate).wait_recv()
        half_copy(owners[1][1], 1, mate).wait_recv()

        def half_rows(owner, half):
            return pl.ds(pl.multiple_of(owner * SHARD + half * HALF, HALF), HALF)

        feats = [
            jnp.concatenate([xt[half_rows(a, 0), :], xt[half_rows(b, 1), :]], axis=0) for a, b in owners
        ]
        tall = mm(rowenc[...], jnp.concatenate(feats, axis=1))
        tall = tall[:128] + tall[128:]
        high, low = split(jnp.concatenate([tall[:, :256], tall[:, 256:]], axis=0))
        grid = mm(jnp.concatenate([high, low, high], axis=1), wx[...])

        masked = []
        for unit, (a, b) in enumerate(owners):
            def mixed(ref, cols=slice(None)):
                return jnp.where(top, eight_of(ref, a)[:, cols], eight_of(ref, b)[:, cols])

            mask = mixed(colmask)
            ahead = mixed(pull)
            vals = [
                jnp.where(
                    top,
                    val[pl.ds(pl.multiple_of(a * 8, 8), 8), k * 128:(k + 1) * 128],
                    val[pl.ds(pl.multiple_of(b * 8, 8), 8), k * 128:(k + 1) * 128],
                )
                for k in range(BAND)
            ]
            grid_a, grid_b = [], []
            for f in range(LOW):
                base = jnp.where(top, gm[a, 8 * f:8 * f + 8, :], gm[b, 8 * f:8 * f + 8, :])
                row = unit * 128 + 8 * f
                grid_a.append(grid[row:row + 8, :128] + 0.81 * base)
                grid_b.append(grid[row:row + 8, 128:] + 0.9 * base)
            thin = []
            for k in range(BAND):
                got = grid_b[k]
                for f in range(k + 1, k + 9):
                    got = jnp.where(vals[k] == f, grid_b[f], got)
                moved = got
                for shift in range(1, 9):
                    moved = jnp.where(ahead == shift, pltpu.roll(got, 128 - shift, 1), moved)
                thin.append(moved)
            for k in range(BAND // 2):
                packed = jnp.where(lane, thin[k], pltpu.roll(thin[k + BAND // 2], BAND, 1))
                stage = s * 2 + unit
                send[stage, pl.ds(k, 8, stride=4), :] = packed
            for f in range(LOW):
                hit = jnp.zeros((8, 128), F32)
                for k in range(max(0, f - 8), min(7, f) + 1):
                    hit = jnp.where(vals[k] == f, mask, hit)
                masked.append(hit * grid_a[f])

        for unit, (a, b) in enumerate(owners):
            for i in range(Y):
                owner = a if i < Y // 2 else b
                tile = send.at[s * 2 + unit, pl.ds(i * 8, 8), :]

                @pl.when(owner * Y + i != dp)
                def _():
                    pltpu.make_async_remote_copy(
                        src_ref=tile,
                        dst_ref=recv.at[dp],
                        send_sem=sum_send,
                        recv_sem=sum_recv,
                        device_id=(owner * Y + i, tensor),
                        device_id_type=MESH,
                    ).start()

                @pl.when(owner * Y + i == dp)
                def _():
                    recv[dp] = send[s * 2 + unit, i * 8:(i + 1) * 8, :]

        high, low = split(jnp.concatenate(masked, axis=0))
        wide = mm(jnp.concatenate([high, low, high], axis=1), coldec[...]) * (-1.0 / FACTOR)
        high, low = split(wide)
        for unit, (a, b) in enumerate(owners):
            here = slice(unit * 128, (unit + 1) * 128)
            rhs[unit, 384:512, :] = high[here]
            rhs[unit, 512:640, :] = low[here]
            rhs[unit, 640:768, :] = high[here]
        for unit, (a, b) in enumerate(owners):
            for half, owner in enumerate((a, b)):
                rows = half_rows(owner, half)
                part = xt[rows, :]
                dec = rowdec[half * HALF:(half + 1) * HALF, :]
                left_side = jnp.concatenate([part, part[:, :128], dec[:, :128], dec], axis=1)
                change = mm(left_side, rhs[unit])
                out_ref[0, rows, :] = (0.81 * m_ref[rows, :].astype(F32) + FACTOR * change).astype(BF16)
        return carry

    lax.fori_loop(0, X, pair_step, 0)

    everyone = recv.at[pl.ds(0, GROUPS - 1)]
    pltpu.make_async_copy(everyone, everyone, sum_recv).wait()
    tot[...] = jnp.zeros((32, 128), F32)
    tot[pl.ds(pl.multiple_of(cy * 8, 8), 8), :] = jnp.sum(recv[...], axis=0)
    behind = eight_of(push, cz)
    vals = [val[pl.ds(pl.multiple_of(cz * 8, 8), 8), k * 128:(k + 1) * 128] for k in range(BAND)]
    sums = []
    for part in range(2):
        for k in range(BAND // 2):
            packed = tot[pl.ds(k, 8, stride=4), :]
            if part:
                packed = pltpu.roll(packed, 128 - BAND, 1)
            full = jnp.zeros((8, 128), F32)
            for shift in range(9):
                moved = pltpu.roll(packed, shift, 1) if shift else packed
                full = jnp.where(behind == shift, moved, full)
            sums.append(full)
    kept = []
    for f in range(LOW):
        hit = jnp.zeros((8, 128), F32)
        for k in range(max(0, f - 8), min(7, f) + 1):
            hit = jnp.where(vals[k] == f, sums[k], hit)
        kept.append(hit)
    high, low = split(jnp.concatenate(kept, axis=0))
    wide = mm(jnp.concatenate([high, low, high], axis=1), coldec[...])
    high, low = split(wide)
    dec = rowdec[pl.ds(pl.multiple_of(cy * 128, 128), 128), :]
    upd_ref[...] = mm(
        jnp.concatenate([dec[:, :128], dec], axis=1), jnp.concatenate([high, low, high], axis=0)
    )

    everyone_sent = recv.at[pl.ds(0, GROUPS - 1)]
    pltpu.make_async_copy(everyone_sent, everyone_sent, sum_send).wait()
    sent = xt.at[pl.ds(0, 7 * SHARD), :]
    pltpu.make_async_copy(sent, sent, gather_send).wait()


def shards(inputs, out_grads, momentum, band):
    consts = [jnp.asarray(c) for c in constants()]
    band_t = jnp.transpose(band, (1, 2, 3, 0))
    hbm = pl.BlockSpec(memory_space=pltpu.HBM)
    vmem = pl.BlockSpec(memory_space=pltpu.VMEM)
    return pl.pallas_call(
        kernel,
        out_shape=(
            pltpu.VMEM(momentum.shape, BF16),
            pltpu.VMEM((128, COLS), F32),
        ),
        in_specs=[hbm] * 6,
        out_specs=(vmem, vmem),
        scratch_shapes=[
            pltpu.VMEM((STEPS, TOK, SHARD), BF16),
            pltpu.VMEM((STEPS, TOK, COLS), BF16),
            pltpu.VMEM((ROWS, COLS), BF16),
            pltpu.VMEM((8, 2, 8, 64), jnp.int32),
            pltpu.VMEM((256, 512), F32),
            pltpu.VMEM((512, 256), F32),
            pltpu.VMEM((256, 512), BF16),
            pltpu.VMEM((512, 256), BF16),
            pltpu.VMEM((512, 256), BF16),
            pltpu.VMEM((384, 512), BF16),
            pltpu.VMEM((ROWS, STEPS * TOK), BF16),
            pltpu.VMEM((64, 2048), F32),
            pltpu.VMEM((64, 128), F32),
            pltpu.VMEM((64, 128), F32),
            pltpu.VMEM((64, 128), F32),
            pltpu.VMEM((768, 256), BF16),
            pltpu.VMEM((2, 768, COLS), BF16),
            pltpu.VMEM((CHUNKS, 128, 128), F32),
            pltpu.VMEM((CHUNKS, 32, 128), F32),
            pltpu.VMEM((GROUPS, 8, 128), F32),
            pltpu.VMEM((32, 128), F32),
            pltpu.SemaphoreType.DMA((6,)),
            pltpu.SemaphoreType.DMA((X,)),
            pltpu.SemaphoreType.DMA,
            pltpu.SemaphoreType.DMA((CHUNKS * 2,)),
            pltpu.SemaphoreType.DMA,
            pltpu.SemaphoreType.DMA,
        ],
        compiler_params=pltpu.CompilerParams(
            collective_id=0, has_side_effects=True, vmem_limit_bytes=40 * 1024 * 1024
        ),
        name="demo_steps",
    )(*[pltpu.with_memory_space_constraint(a, pltpu.HBM) for a in (inputs, out_grads, momentum, band_t, *consts)])


def solution(mesh):
    return jax.shard_map(
        shards,
        mesh=mesh,
        in_specs=(
            P(None, "dp", "tensor"),
            P(None, "dp", "tensor"),
            P("dp", None, "tensor"),
            P(None, "tensor", None, None),
        ),
        out_specs=(P("dp", None, "tensor"), P("dp", "tensor")),
        check_vma=False,
    )
```

```python
import functools
import math

import jax
import jax.numpy as jnp
import ml_dtypes
import numpy as np
from jax import lax
from jax.experimental import pallas as pl
from jax.experimental.pallas import tpu as pltpu
from jax.sharding import PartitionSpec as P

MESH = pl.DeviceIdType.MESH
F32 = jnp.float32
BF16 = jnp.bfloat16
SPAN = 64
LOW = 16
BAND = 8
TOK = 128
ROWS = 4096
COLS = 512
SHARD = 512
STEPS = 2
X = 4
GROUPS = 32
Y = 4
HALF = SHARD // 2
CHUNKS = 8
PARTS = 8
FACTOR = 1.0 / math.sqrt(TOK)


def split_const(table):
    high = table.astype(ml_dtypes.bfloat16).astype(np.float32)
    return high, (table - high).astype(ml_dtypes.bfloat16).astype(np.float32)


def low_rows():
    freq = np.arange(LOW)[:, None]
    place = np.arange(SPAN)[None, :]
    table = np.sqrt(2.0 / SPAN) * np.cos(math.pi * (2.0 * place + 1.0) * freq / (2.0 * SPAN))
    table[0] /= math.sqrt(2.0)
    return table.astype(np.float32)


def constants():
    low = low_rows()
    four = np.zeros((LOW, 4, 4, SPAN), np.float32)
    enc = np.zeros((LOW, 8, 8, SPAN), np.float32)
    col = np.zeros((8, SPAN, 8, LOW), np.float32)
    for block in range(8):
        enc[:, block, block, :] = low
        col[block, :, block, :] = low.T
        if block < 4:
            four[:, block, block, :] = low
    rowenc = np.concatenate(split_const(four.reshape(64, 256)), axis=0)
    rowdec = np.concatenate(split_const(enc.reshape(128, 512).T), axis=1)
    colenc = np.concatenate(split_const(col.reshape(512, 128)), axis=1)
    high, lower = split_const(col.reshape(512, 128).T)
    zero = np.zeros((64, 256), np.float32)
    first = [high[:64, :256], lower[:64, :256], high[:64, :256], zero]
    second = [lower[64:, 256:], high[64:, 256:], zero, high[64:, 256:]]
    coldec = np.concatenate([np.concatenate(first, axis=0), np.concatenate(second, axis=0)], axis=1)
    return rowenc, rowdec, colenc, coldec


def split(a):
    high = a.astype(BF16)
    low = (a - high.astype(F32)).astype(BF16)
    return high, low


def mm(a, b):
    return jnp.dot(a, b, preferred_element_type=F32)


def widen(grids, coldec):
    lane = lax.broadcasted_iota(jnp.int32, grids.shape, 1) < 64
    turned = pltpu.roll(grids, 64, 1)
    high, low = split(grids)
    first = jnp.concatenate([jnp.where(lane, grids, turned).astype(BF16), low], axis=1)
    second = jnp.concatenate([jnp.where(lane, turned, grids).astype(BF16), low], axis=1)
    return jnp.concatenate([mm(first, coldec[:, :256]), mm(second, coldec[:, 256:])], axis=1)


def kernel(
    x_hbm, d_hbm, m_hbm, band_hbm, rowenc_hbm, rowdec_hbm, colenc_hbm, coldec_hbm,
    out_ref, recv, own, coldec, rowdec,
    xin, din, m_ref, band_ref, rowenc_in, rowdec_in, colenc_in, coldec_in, rowenc, colenc,
    xt, val, colmask, pull, push, wx, rhs, gm, kept, send,
    load_sem, m_sem, gather_send, gather_recv, sum_send, sum_recv,
):
    dp = lax.axis_index("dp")
    tensor = lax.axis_index("tensor")
    cx = tensor // 2
    core = tensor % 2
    cz = dp // Y
    cy = dp % Y

    def tensor_of(hop, other):
        return 2 * ((cx + hop) % X) + (core + other) % 2

    mate = tensor_of(0, 1)
    right = tensor_of(1, 0)
    left = tensor_of(X - 1, 0)

    def load(src, dst, n):
        copy = pltpu.make_async_copy(src, dst, load_sem.at[n])
        copy.start()
        return copy

    x_loads = [
        load(x_hbm.at[:, :, half * 256:(half + 1) * 256], xin.at[:, :, half * 256:(half + 1) * 256], half)
        for half in range(2)
    ]
    barrier = pltpu.get_barrier_semaphore()
    for peer in (mate, right, left):
        pl.semaphore_signal(barrier, inc=1, device_id=(dp, peer), device_id_type=MESH)
    colenc_load = load(colenc_hbm, colenc_in, 2)
    d_load = load(d_hbm, din, 3)
    band_load = load(band_hbm, band_ref, 4)
    rowenc_load = load(rowenc_hbm, rowenc_in, 5)
    coldec_load = load(coldec_hbm, coldec_in, 6)
    rowdec_load = load(rowdec_hbm, rowdec_in, 7)

    def m_copy(p):
        rows = pl.ds(pl.multiple_of(p * 2 * SHARD, 2 * SHARD), 2 * SHARD)
        return pltpu.make_async_copy(m_hbm.at[0, rows, :], m_ref.at[rows, :], m_sem.at[p])

    for p in range(X):
        m_copy(p).start()

    def greet(i, carry):
        pl.semaphore_signal(
            barrier, inc=1, device_id=((dp + i) % GROUPS, tensor), device_id_type=MESH
        )
        return carry

    lax.fori_loop(1, GROUPS, greet, 0)

    def half_copy(owner, half, target):
        rows = pl.ds(pl.multiple_of(owner * SHARD + half * HALF, HALF), HALF)
        return pltpu.make_async_remote_copy(
            src_ref=xt.at[rows, :],
            dst_ref=xt.at[rows, :],
            send_sem=gather_send,
            recv_sem=gather_recv.at[owner * 2 + half],
            device_id=(dp, target),
            device_id_type=MESH,
        )

    def turn(half):
        x_loads[half].wait()
        rows = pl.ds(pl.multiple_of(tensor * SHARD + half * HALF, HALF), HALF)
        for step in range(STEPS):
            xt[rows, step * TOK:(step + 1) * TOK] = xin[step, :, half * HALF:(half + 1) * HALF].T

    turn(0)
    pl.semaphore_wait(barrier, 3 + GROUPS - 1)
    half_copy(tensor, 0, right).start()
    turn(1)
    half_copy(tensor, 1, left).start()
    half_copy(tensor, 0, mate).start()
    half_copy(tensor, 1, mate).start()
    half_copy(tensor, 1, right).start()
    half_copy(tensor, 0, left).start()

    colenc_load.wait()
    colenc[...] = colenc_in[...].astype(BF16)
    d_load.wait()
    both = mm(jnp.concatenate([din[0], din[1]], axis=0), colenc[...])
    hats = (both[:, :128] + both[:, 128:]) * FACTOR
    table = jnp.concatenate(
        [jnp.concatenate([0.9 * hats[:128], hats[:128]], axis=1), jnp.concatenate([hats[128:], hats[128:]], axis=1)],
        axis=0,
    )
    high, low = split(table)
    wx[0:256, :] = high
    wx[256:512, :] = high
    wx[512:768, :] = low
    high, low = split(0.9 * din[0].astype(F32))
    for unit in range(2):
        rhs[unit, 0:128, :] = high
        rhs[unit, 128:256, :] = din[1]
        rhs[unit, 256:384, :] = low

    band_load.wait()
    picks = band_ref[...].reshape(128, 64).astype(F32).T.astype(BF16)
    away = lax.broadcasted_iota(jnp.int32, (128, 128), 0) - lax.broadcasted_iota(jnp.int32, (128, 128), 1) // LOW * 16
    for n in range(2 * BAND):
        val[:, n * 128:(n + 1) * 128] = mm(picks, (away == n).astype(F32).astype(BF16))
    place = (lax.broadcasted_iota(jnp.int32, (64, 128), 1) % LOW).astype(F32)
    seen = jnp.zeros((64, 128), F32)
    ahead = jnp.zeros((64, 128), F32)
    back = jnp.full((64, 128), -1.0, F32)
    for k in range(BAND):
        freq = val[:, (BAND + k) * 128:(BAND + k + 1) * 128]
        seen = jnp.where(freq == place, 1.0, seen)
        back = jnp.where(freq == place, place - k, back)
        ahead = jnp.where(place == k, freq - k, ahead)
    colmask[...] = seen
    pull[...] = ahead
    push[...] = back

    rowenc_load.wait()
    rowenc[...] = rowenc_in[...].astype(BF16)

    def encode(halves):
        wide = mm(rowenc[...], jnp.concatenate(halves, axis=1))
        wide = wide[:64] + wide[64:]
        size = halves[0].shape[1]
        return split(jnp.concatenate([wide[:, n * size:(n + 1) * size] for n in range(len(halves))], axis=0))

    def momentum_step(p, carry):
        m_copy(p).wait()
        high, low = encode(
            [m_ref[pl.ds(pl.multiple_of(p * 2 * SHARD + n * HALF, HALF), HALF), :] for n in range(4)]
        )
        both = mm(jnp.concatenate([high, low], axis=0), colenc[...])
        gm[p] = both[:256, :128] + both[:256, 128:] + both[256:, :128]
        return carry

    lax.fori_loop(0, X, momentum_step, 0)
    coldec_load.wait()
    coldec[...] = coldec_in[...].astype(BF16)
    rowdec_load.wait()
    rowdec[...] = rowdec_in[...].astype(BF16)

    top = lax.broadcasted_iota(jnp.int32, (8, 128), 0) < 4
    lane = lax.broadcasted_iota(jnp.int32, (8, 128), 1) % LOW < BAND

    def eight_of(ref, owner):
        return ref[pl.ds(pl.multiple_of(owner * 8, 8), 8), :]

    def owners_of(s):
        hop_a = jnp.where(s == 0, 0, jnp.where(s == 1, X - 1, jnp.where(s == 2, 1, 2)))
        hop_b = jnp.where(s == 0, 0, jnp.where(s == 1, 1, jnp.where(s == 2, X - 1, 2)))
        return [(tensor_of(hop_a, other), tensor_of(hop_b, other)) for other in range(2)]

    def half_rows(owner, half):
        return pl.ds(pl.multiple_of(owner * SHARD + half * HALF, HALF), HALF)

    def write_pair(s):
        grids = jnp.concatenate([kept[s * 2], kept[s * 2 + 1]], axis=0)
        wide = widen(grids, coldec[...]) * (-1.0 / FACTOR)
        high, low = split(wide)
        for unit, (a, b) in enumerate(owners_of(s)):
            here = slice(unit * 128, (unit + 1) * 128)
            rhs[unit, 384:512, :] = high[here]
            rhs[unit, 512:640, :] = low[here]
            rhs[unit, 640:768, :] = high[here]
        for unit, (a, b) in enumerate(owners_of(s)):
            for half, owner in enumerate((a, b)):
                rows = half_rows(owner, half)
                part = xt[rows, :]
                dec = rowdec[half * HALF:(half + 1) * HALF, :]
                left_side = jnp.concatenate([part, part[:, :128], dec[:, :128], dec], axis=1)
                change = mm(left_side, rhs[unit])
                out_ref[0, rows, :] = (0.81 * m_ref[rows, :].astype(F32) + FACTOR * change).astype(BF16)

    def pair_step(s, carry):
        owners = owners_of(s)

        @pl.when(s > 0)
        def _():
            half_copy(owners[0][0], 0, mate).wait_recv()
            half_copy(owners[0][0], 0, mate).start()

            @pl.when(s == 1)
            def _():
                half_copy(left, 0, right).start()

            half_copy(owners[0][1], 1, mate).wait_recv()
            half_copy(owners[0][1], 1, mate).start()

            @pl.when(s == 1)
            def _():
                half_copy(right, 1, left).start()

            write_pair(s - 1)

        half_copy(owners[1][0], 0, mate).wait_recv()
        half_copy(owners[1][1], 1, mate).wait_recv()

        quarters = [(a, 0) if half == 0 else (b, 1) for a, b in owners for half in range(2)]
        high, low = encode([xt[half_rows(owner, half), :] for owner, half in quarters])
        grid = mm(jnp.concatenate([high, low, high], axis=1), wx[...])
        grid_a, grid_b = [], []
        for n, (owner, half) in enumerate(quarters):
            start = pl.multiple_of((owner % 2) * 128 + half * 64, 64)
            base = gm[owner // 2, pl.ds(start, 64), :]
            grid_a.append(grid[n * 64:(n + 1) * 64, :128] + 0.81 * base)
            grid_b.append(grid[n * 64:(n + 1) * 64, 128:] + 0.9 * base)

        def by_frequency(first, second):
            tiles = []
            for n in range(LOW // 2):
                one, two = first[8 * n:8 * n + 8], second[8 * n:8 * n + 8]
                tiles.append(jnp.where(top, one, pltpu.roll(two, 4, 0)))
                tiles.append(jnp.where(top, pltpu.roll(one, 4, 0), two))
            return tiles

        for unit, (a, b) in enumerate(owners):
            def mixed(ref, cols=slice(None)):
                return jnp.where(top, eight_of(ref, a)[:, cols], eight_of(ref, b)[:, cols])

            mask = mixed(colmask)
            ahead = mixed(pull)
            vals = [
                jnp.where(
                    top,
                    val[pl.ds(pl.multiple_of(a * 8, 8), 8), k * 128:(k + 1) * 128],
                    val[pl.ds(pl.multiple_of(b * 8, 8), 8), k * 128:(k + 1) * 128],
                )
                for k in range(BAND)
            ]
            for_a = by_frequency(grid_a[2 * unit], grid_a[2 * unit + 1])
            for_b = by_frequency(grid_b[2 * unit], grid_b[2 * unit + 1])
            thin = []
            for k in range(BAND):
                got = for_b[k]
                for f in range(k + 1, k + 9):
                    got = jnp.where(vals[k] == f, for_b[f], got)
                moved = got
                for shift in range(1, 9):
                    moved = jnp.where(ahead == shift, pltpu.roll(got, 128 - shift, 1), moved)
                thin.append(moved)
            for k in range(BAND // 2):
                packed = jnp.where(lane, thin[k], pltpu.roll(thin[k + BAND // 2], BAND, 1))
                stage = s * 2 + unit
                send[stage, pl.ds(k, 8, stride=4), :] = packed
            for f in range(LOW):
                hit = jnp.zeros((8, 128), F32)
                for k in range(max(0, f - 8), min(7, f) + 1):
                    hit = jnp.where(vals[k] == f, mask, hit)
                kept[s * 2 + unit, 8 * f:8 * f + 8, :] = hit * for_a[f]

        for unit, (a, b) in enumerate(owners):
            for i in range(Y):
                owner = a if i < Y // 2 else b
                tile = send.at[s * 2 + unit, pl.ds(i * 8, 8), :]

                @pl.when(owner * Y + i != dp)
                def _():
                    pltpu.make_async_remote_copy(
                        src_ref=tile,
                        dst_ref=recv.at[dp],
                        send_sem=sum_send,
                        recv_sem=sum_recv,
                        device_id=(owner * Y + i, tensor),
                        device_id_type=MESH,
                    ).start()

                @pl.when(owner * Y + i == dp)
                def _():
                    recv[dp] = send[s * 2 + unit, i * 8:(i + 1) * 8, :]

        return carry

    lax.fori_loop(0, X, pair_step, 0)
    write_pair(X - 1)

    for k in range(BAND):
        own[k] = val[pl.ds(pl.multiple_of(cz * 8, 8), 8), k * 128:(k + 1) * 128]
    own[BAND] = eight_of(push, cz)
    everyone = recv.at[pl.ds(0, GROUPS - 1)]
    pltpu.make_async_copy(everyone, everyone, sum_recv).wait()
    everyone_sent = recv.at[pl.ds(0, GROUPS - 1)]
    pltpu.make_async_copy(everyone_sent, everyone_sent, sum_send).wait()
    sent = xt.at[pl.ds(0, 7 * SHARD), :]
    pltpu.make_async_copy(sent, sent, gather_send).wait()


def finish(new_ref, recv, own, coldec, rowdec, out_hbm, upd_hbm, tot, upd, sem):
    cy = lax.axis_index("dp") % Y
    rows = ROWS // PARTS
    copies = [
        pltpu.make_async_copy(
            new_ref.at[0, pl.ds(n * rows, rows), :], out_hbm.at[0, pl.ds(n * rows, rows), :], sem.at[n]
        )
        for n in range(PARTS)
    ]
    for copy in copies:
        copy.start()
    tot[...] = jnp.zeros((32, 128), F32)
    tot[pl.ds(pl.multiple_of(cy * 8, 8), 8), :] = jnp.sum(recv[...], axis=0)
    behind = own[BAND]
    vals = [own[k] for k in range(BAND)]
    sums = []
    for part in range(2):
        for k in range(BAND // 2):
            packed = tot[pl.ds(k, 8, stride=4), :]
            if part:
                packed = pltpu.roll(packed, 128 - BAND, 1)
            full = jnp.zeros((8, 128), F32)
            for shift in range(9):
                moved = pltpu.roll(packed, shift, 1) if shift else packed
                full = jnp.where(behind == shift, moved, full)
            sums.append(full)
    kept = []
    for f in range(LOW):
        hit = jnp.zeros((8, 128), F32)
        for k in range(max(0, f - 8), min(7, f) + 1):
            hit = jnp.where(vals[k] == f, sums[k], hit)
        kept.append(hit)
    wide = widen(jnp.concatenate(kept, axis=0), coldec[...])
    high, low = split(wide)
    dec = rowdec[pl.ds(pl.multiple_of(cy * 128, 128), 128), :]
    upd[...] = mm(
        jnp.concatenate([dec[:, :128], dec], axis=1), jnp.concatenate([high, low, high], axis=0)
    )

    last = pltpu.make_async_copy(upd, upd_hbm, sem.at[PARTS])
    last.start()
    for copy in copies:
        copy.wait()
    last.wait()


def shards(inputs, out_grads, momentum, band):
    consts = [jnp.asarray(c) for c in constants()]
    band_t = jnp.transpose(band, (1, 2, 3, 0))
    hbm = pl.BlockSpec(memory_space=pltpu.HBM)
    vmem = pl.BlockSpec(memory_space=pltpu.VMEM)
    parts = pl.pallas_call(
        kernel,
        out_shape=(
            pltpu.VMEM(momentum.shape, BF16),
            pltpu.VMEM((GROUPS, 8, 128), F32),
            pltpu.VMEM((BAND + 1, 8, 128), F32),
            pltpu.VMEM((256, COLS), BF16),
            pltpu.VMEM((SHARD, 256), BF16),
        ),
        in_specs=[hbm] * 8,
        out_specs=(vmem,) * 5,
        scratch_shapes=[
            pltpu.VMEM((STEPS, TOK, SHARD), BF16),
            pltpu.VMEM((STEPS, TOK, COLS), BF16),
            pltpu.VMEM((ROWS, COLS), BF16),
            pltpu.VMEM((8, 2, 8, 64), jnp.int32),
            pltpu.VMEM((128, 256), F32),
            pltpu.VMEM((512, 256), F32),
            pltpu.VMEM((512, 256), F32),
            pltpu.VMEM((256, 512), F32),
            pltpu.VMEM((128, 256), BF16),
            pltpu.VMEM((512, 256), BF16),
            pltpu.VMEM((ROWS, STEPS * TOK), BF16),
            pltpu.VMEM((64, 2048), F32),
            pltpu.VMEM((64, 128), F32),
            pltpu.VMEM((64, 128), F32),
            pltpu.VMEM((64, 128), F32),
            pltpu.VMEM((768, 256), BF16),
            pltpu.VMEM((2, 768, COLS), BF16),
            pltpu.VMEM((X, 256, 128), F32),
            pltpu.VMEM((CHUNKS, 128, 128), F32),
            pltpu.VMEM((CHUNKS, 32, 128), F32),
            pltpu.SemaphoreType.DMA((8,)),
            pltpu.SemaphoreType.DMA((X,)),
            pltpu.SemaphoreType.DMA,
            pltpu.SemaphoreType.DMA((CHUNKS * 2,)),
            pltpu.SemaphoreType.DMA,
            pltpu.SemaphoreType.DMA,
        ],
        compiler_params=pltpu.CompilerParams(
            collective_id=0, has_side_effects=True, vmem_limit_bytes=40 * 1024 * 1024
        ),
        name="demo_steps",
    )(*[pltpu.with_memory_space_constraint(a, pltpu.HBM) for a in (inputs, out_grads, momentum, band_t, *consts)])
    parts = [pltpu.with_memory_space_constraint(a, pltpu.VMEM) for a in parts]
    return pl.pallas_call(
        finish,
        out_shape=(pltpu.HBM(momentum.shape, BF16), pltpu.HBM((128, COLS), F32)),
        in_specs=[vmem] * 5,
        out_specs=(hbm, hbm),
        scratch_shapes=[
            pltpu.VMEM((32, 128), F32),
            pltpu.VMEM((128, COLS), F32),
            pltpu.SemaphoreType.DMA((PARTS + 1,)),
        ],
        compiler_params=pltpu.CompilerParams(vmem_limit_bytes=8 * 1024 * 1024),
        name="demo_finish",
    )(*parts)


def solution(mesh):
    return jax.shard_map(
        shards,
        mesh=mesh,
        in_specs=(
            P(None, "dp", "tensor"),
            P(None, "dp", "tensor"),
            P("dp", None, "tensor"),
            P(None, "tensor", None, None),
        ),
        out_specs=(P("dp", None, "tensor"), P("dp", "tensor")),
        check_vma=False,
    )
```

```python
import functools
import math

import jax
import jax.numpy as jnp
import ml_dtypes
import numpy as np
from jax import lax
from jax.experimental import pallas as pl
from jax.experimental.pallas import tpu as pltpu
from jax.sharding import PartitionSpec as P

MESH = pl.DeviceIdType.MESH
F32 = jnp.float32
BF16 = jnp.bfloat16
SPAN = 64
LOW = 16
BAND = 8
TOK = 128
ROWS = 4096
COLS = 512
SHARD = 512
STEPS = 2
X = 4
GROUPS = 32
Y = 4
HALF = SHARD // 2
CHUNKS = 8
PARTS = 8
FACTOR = 1.0 / math.sqrt(TOK)


def split_const(table):
    high = table.astype(ml_dtypes.bfloat16).astype(np.float32)
    return high, (table - high).astype(ml_dtypes.bfloat16).astype(np.float32)


def low_rows():
    freq = np.arange(LOW)[:, None]
    place = np.arange(SPAN)[None, :]
    table = np.sqrt(2.0 / SPAN) * np.cos(math.pi * (2.0 * place + 1.0) * freq / (2.0 * SPAN))
    table[0] /= math.sqrt(2.0)
    return table.astype(np.float32)


def constants():
    low = low_rows()
    four = np.zeros((LOW, 4, 4, SPAN), np.float32)
    enc = np.zeros((LOW, 8, 8, SPAN), np.float32)
    col = np.zeros((8, SPAN, 8, LOW), np.float32)
    for block in range(8):
        enc[:, block, block, :] = low
        col[block, :, block, :] = low.T
        if block < 4:
            four[:, block, block, :] = low
    rowenc = np.concatenate(split_const(four.reshape(64, 256)), axis=0)
    rowdec = np.concatenate(split_const(enc.reshape(128, 512).T), axis=1)
    colenc = np.concatenate(split_const(col.reshape(512, 128)), axis=1)
    high, lower = split_const(col.reshape(512, 128).T)
    zero = np.zeros((64, 256), np.float32)
    first = [high[:64, :256], lower[:64, :256], high[:64, :256], zero]
    second = [lower[64:, 256:], high[64:, 256:], zero, high[64:, 256:]]
    coldec = np.concatenate([np.concatenate(first, axis=0), np.concatenate(second, axis=0)], axis=1)
    return rowenc, rowdec, colenc, coldec


def split(a):
    high = a.astype(BF16)
    low = (a - high.astype(F32)).astype(BF16)
    return high, low


def mm(a, b):
    return jnp.dot(a, b, preferred_element_type=F32)


def widen(grids, coldec):
    lane = lax.broadcasted_iota(jnp.int32, grids.shape, 1) < 64
    turned = pltpu.roll(grids, 64, 1)
    high, low = split(grids)
    first = jnp.concatenate([jnp.where(lane, grids, turned).astype(BF16), low], axis=1)
    second = jnp.concatenate([jnp.where(lane, turned, grids).astype(BF16), low], axis=1)
    return jnp.concatenate([mm(first, coldec[:, :256]), mm(second, coldec[:, 256:])], axis=1)


def kernel(
    x_hbm, d_hbm, m_hbm, band_hbm, rowenc_hbm, rowdec_hbm, colenc_hbm, coldec_hbm,
    out_ref, recv, own, coldec, rowdec,
    xin, din, m_ref, band_ref, rowenc_in, rowdec_in, colenc_in, coldec_in, rowenc, colenc,
    xt, val, colmask, pull, push, wx, rhs, gm, kept, send, gm_mate, val_mate, pull_mate, mask_mate,
    load_sem, m_sem, gather_send, gather_recv, sum_send, sum_recv, swap_send, swap_recv,
):
    dp = lax.axis_index("dp")
    tensor = lax.axis_index("tensor")
    cx = tensor // 2
    core = tensor % 2
    cz = dp // Y
    cy = dp % Y

    def tensor_of(hop, other):
        return 2 * ((cx + hop) % X) + (core + other) % 2

    mate = tensor_of(0, 1)
    right = tensor_of(1, 0)
    left = tensor_of(X - 1, 0)
    far = tensor_of(2, 0)
    far_mate = tensor_of(2, 1)
    crossed = cz == far_mate

    def load(src, dst, n):
        copy = pltpu.make_async_copy(src, dst, load_sem.at[n])
        copy.start()
        return copy

    x_loads = [
        load(x_hbm.at[:, :, half * 256:(half + 1) * 256], xin.at[:, :, half * 256:(half + 1) * 256], half)
        for half in range(2)
    ]
    barrier = pltpu.get_barrier_semaphore()
    for peer in (mate, right, left):
        pl.semaphore_signal(barrier, inc=1, device_id=(dp, peer), device_id_type=MESH)
    colenc_load = load(colenc_hbm, colenc_in, 2)
    d_load = load(d_hbm, din, 3)
    band_load = load(band_hbm, band_ref, 4)
    rowenc_load = load(rowenc_hbm, rowenc_in, 5)
    coldec_load = load(coldec_hbm, coldec_in, 6)
    rowdec_load = load(rowdec_hbm, rowdec_in, 7)

    def m_copy(p):
        rows = pl.ds(pl.multiple_of(p * 2 * SHARD, 2 * SHARD), 2 * SHARD)
        return pltpu.make_async_copy(m_hbm.at[0, rows, :], m_ref.at[rows, :], m_sem.at[p])

    for p in range(X):
        m_copy(p).start()

    def greet(i, carry):
        pl.semaphore_signal(
            barrier, inc=1, device_id=((dp + i) % GROUPS, tensor), device_id_type=MESH
        )
        return carry

    lax.fori_loop(1, GROUPS, greet, 0)

    @pl.when(crossed)
    def _():
        def greet_mates(i, carry):
            pl.semaphore_signal(
                barrier, inc=1, device_id=((dp + i) % GROUPS, mate), device_id_type=MESH
            )
            return carry

        lax.fori_loop(1, GROUPS, greet_mates, 0)

    def half_copy(owner, half, target):
        rows = pl.ds(pl.multiple_of(owner * SHARD + half * HALF, HALF), HALF)
        return pltpu.make_async_remote_copy(
            src_ref=xt.at[rows, :],
            dst_ref=xt.at[rows, :],
            send_sem=gather_send,
            recv_sem=gather_recv.at[owner * 2 + half],
            device_id=(dp, target),
            device_id_type=MESH,
        )

    def turn(half):
        x_loads[half].wait()
        rows = pl.ds(pl.multiple_of(tensor * SHARD + half * HALF, HALF), HALF)
        for step in range(STEPS):
            xt[rows, step * TOK:(step + 1) * TOK] = xin[step, :, half * HALF:(half + 1) * HALF].T

    turn(0)
    pl.semaphore_wait(barrier, 3 + GROUPS - 1 + jnp.where(cz == far, Y - 1, Y))
    half_copy(tensor, 0, right).start()
    turn(1)
    half_copy(tensor, 1, left).start()
    half_copy(tensor, 0, mate).start()
    half_copy(tensor, 1, mate).start()
    half_copy(tensor, 1, right).start()
    half_copy(tensor, 0, left).start()

    colenc_load.wait()
    colenc[...] = colenc_in[...].astype(BF16)
    d_load.wait()
    both = mm(jnp.concatenate([din[0], din[1]], axis=0), colenc[...])
    hats = (both[:, :128] + both[:, 128:]) * FACTOR
    table = jnp.concatenate(
        [jnp.concatenate([0.9 * hats[:128], hats[:128]], axis=1), jnp.concatenate([hats[128:], hats[128:]], axis=1)],
        axis=0,
    )
    high, low = split(table)
    wx[0:256, 0:256] = high
    wx[256:512, 0:256] = high
    wx[512:768, 0:256] = low
    high, low = split(0.9 * din[0].astype(F32))
    for unit in range(2):
        rhs[unit, 0:128, :] = high
        rhs[unit, 128:256, :] = din[1]
        rhs[unit, 256:384, :] = low

    band_load.wait()
    picks = band_ref[...].reshape(128, 64).astype(F32).T.astype(BF16)
    away = lax.broadcasted_iota(jnp.int32, (128, 128), 0) - lax.broadcasted_iota(jnp.int32, (128, 128), 1) // LOW * 16
    for n in range(2 * BAND):
        val[:, n * 128:(n + 1) * 128] = mm(picks, (away == n).astype(F32).astype(BF16))
    place = (lax.broadcasted_iota(jnp.int32, (64, 128), 1) % LOW).astype(F32)
    seen = jnp.zeros((64, 128), F32)
    ahead = jnp.zeros((64, 128), F32)
    back = jnp.full((64, 128), -1.0, F32)
    for k in range(BAND):
        freq = val[:, (BAND + k) * 128:(BAND + k + 1) * 128]
        seen = jnp.where(freq == place, 1.0, seen)
        back = jnp.where(freq == place, place - k, back)
        ahead = jnp.where(place == k, freq - k, ahead)
    colmask[...] = seen
    pull[...] = ahead
    push[...] = back

    rowenc_load.wait()
    rowenc[...] = rowenc_in[...].astype(BF16)

    def encode(halves):
        wide = mm(rowenc[...], jnp.concatenate(halves, axis=1))
        wide = wide[:64] + wide[64:]
        size = halves[0].shape[1]
        return split(jnp.concatenate([wide[:, n * size:(n + 1) * size] for n in range(len(halves))], axis=0))

    def momentum_step(p, carry):
        m_copy(p).wait()
        high, low = encode(
            [m_ref[pl.ds(pl.multiple_of(p * 2 * SHARD + n * HALF, HALF), HALF), :] for n in range(4)]
        )
        both = mm(jnp.concatenate([high, low], axis=0), colenc[...])
        gm[p] = both[:256, :128] + both[:256, 128:] + both[256:, :128]
        return carry

    lax.fori_loop(0, X, momentum_step, 0)

    def swap(src, dst, n):
        return pltpu.make_async_remote_copy(
            src_ref=src, dst_ref=dst, send_sem=swap_send.at[n], recv_sem=swap_recv.at[n],
            device_id=(dp, mate), device_id_type=MESH,
        )

    mate_rows = pl.ds(pl.multiple_of(far_mate * 8, 8), 8)
    swaps = [
        swap(wx.at[:, 128:256], wx.at[:, 256:384], 0),
        swap(gm.at[far_mate // 2, pl.ds(pl.multiple_of(far_mate % 2 * 128, 128), 128), :], gm_mate, 1),
        swap(val.at[mate_rows, 0:1024], val_mate, 2),
        swap(pull.at[mate_rows, :], pull_mate, 3),
        swap(colmask.at[mate_rows, :], mask_mate, 4),
    ]
    for copy in swaps:
        copy.start()
    coldec_load.wait()
    coldec[...] = coldec_in[...].astype(BF16)
    rowdec_load.wait()
    rowdec[...] = rowdec_in[...].astype(BF16)

    top = lax.broadcasted_iota(jnp.int32, (8, 128), 0) < 4
    lane = lax.broadcasted_iota(jnp.int32, (8, 128), 1) % LOW < BAND

    def eight_of(ref, owner):
        return ref[pl.ds(pl.multiple_of(owner * 8, 8), 8), :]

    def owners_of(s):
        hop_a = jnp.where(s == 0, 0, jnp.where(s == 1, X - 1, jnp.where(s == 2, 1, 2)))
        hop_b = jnp.where(s == 0, 0, jnp.where(s == 1, 1, jnp.where(s == 2, X - 1, 2)))
        return [(tensor_of(hop_a, other), tensor_of(hop_b, other)) for other in range(2)]

    def half_rows(owner, half):
        return pl.ds(pl.multiple_of(owner * SHARD + half * HALF, HALF), HALF)

    def write_pair(s):
        grids = jnp.concatenate([kept[s * 2], kept[s * 2 + 1]], axis=0)
        wide = widen(grids, coldec[...]) * (-1.0 / FACTOR)
        high, low = split(wide)
        for unit, (a, b) in enumerate(owners_of(s)):
            here = slice(unit * 128, (unit + 1) * 128)
            rhs[unit, 384:512, :] = high[here]
            rhs[unit, 512:640, :] = low[here]
            rhs[unit, 640:768, :] = high[here]
        for unit, (a, b) in enumerate(owners_of(s)):
            for half, owner in enumerate((a, b)):
                rows = half_rows(owner, half)
                part = xt[rows, :]
                dec = rowdec[half * HALF:(half + 1) * HALF, :]
                left_side = jnp.concatenate([part, part[:, :128], dec[:, :128], dec], axis=1)
                change = mm(left_side, rhs[unit])
                out_ref[0, rows, :] = (0.81 * m_ref[rows, :].astype(F32) + FACTOR * change).astype(BF16)

    def by_frequency(first, second):
        tiles = []
        for n in range(LOW // 2):
            one, two = first[8 * n:8 * n + 8], second[8 * n:8 * n + 8]
            tiles.append(jnp.where(top, one, pltpu.roll(two, 4, 0)))
            tiles.append(jnp.where(top, pltpu.roll(one, 4, 0), two))
        return tiles

    def picks_of(a, b):
        def mixed(ref, cols=slice(0, 128)):
            rows_a = pl.ds(pl.multiple_of(a * 8, 8), 8)
            rows_b = pl.ds(pl.multiple_of(b * 8, 8), 8)
            return jnp.where(top, ref[rows_a, cols], ref[rows_b, cols])

        return mixed(colmask), mixed(pull), [mixed(val, slice(k * 128, (k + 1) * 128)) for k in range(BAND)]

    def pack(stage, tiles, picks):
        mask, ahead, vals = picks
        thin = []
        for k in range(BAND):
            got = tiles[k]
            for f in range(k + 1, k + 9):
                got = jnp.where(vals[k] == f, tiles[f], got)
            moved = got
            for shift in range(1, 9):
                moved = jnp.where(ahead == shift, pltpu.roll(got, 128 - shift, 1), moved)
            thin.append(moved)
        for k in range(BAND // 2):
            packed = jnp.where(lane, thin[k], pltpu.roll(thin[k + BAND // 2], BAND, 1))
            send[stage, pl.ds(k, 8, stride=4), :] = packed

    def keep(unit, tiles, picks):
        mask, ahead, vals = picks
        for f in range(LOW):
            hit = jnp.zeros((8, 128), F32)
            for k in range(max(0, f - 8), min(7, f) + 1):
                hit = jnp.where(vals[k] == f, mask, hit)
            kept[unit, 8 * f:8 * f + 8, :] = hit * tiles[f]

    def own_base(owner, half):
        start = pl.multiple_of((owner % 2) * 128 + half * 64, 64)
        return gm[owner // 2, pl.ds(start, 64), :]

    def ship(stage, owner, i, column):
        return pltpu.make_async_remote_copy(
            src_ref=send.at[stage, pl.ds(i * 8, 8), :],
            dst_ref=recv.at[dp],
            send_sem=sum_send,
            recv_sem=sum_recv,
            device_id=(owner * Y + i, column),
            device_id_type=MESH,
        )

    def ship_own(stage, a, b):
        for i in range(Y):
            owner = a if i < Y // 2 else b

            @pl.when(owner * Y + i != dp)
            def _():
                ship(stage, owner, i, tensor).start()

            @pl.when(owner * Y + i == dp)
            def _():
                recv[dp] = send[stage, i * 8:(i + 1) * 8, :]

    def pair_step(s, carry):
        owners = owners_of(s)

        @pl.when(s > 0)
        def _():
            half_copy(owners[0][0], 0, mate).wait_recv()
            half_copy(owners[0][0], 0, mate).start()

            @pl.when(s == 1)
            def _():
                half_copy(left, 0, right).start()

            half_copy(owners[0][1], 1, mate).wait_recv()
            half_copy(owners[0][1], 1, mate).start()

            @pl.when(s == 1)
            def _():
                half_copy(right, 1, left).start()

            write_pair(s - 1)

        half_copy(owners[1][0], 0, mate).wait_recv()
        half_copy(owners[1][1], 1, mate).wait_recv()

        quarters = [(a, 0) if half == 0 else (b, 1) for a, b in owners for half in range(2)]
        high, low = encode([xt[half_rows(owner, half), :] for owner, half in quarters])
        grid = mm(jnp.concatenate([high, low, high], axis=1), wx[:, 0:256])
        grid_a, grid_b = [], []
        for n, (owner, half) in enumerate(quarters):
            base = own_base(owner, half)
            grid_a.append(grid[n * 64:(n + 1) * 64, :128] + 0.81 * base)
            grid_b.append(grid[n * 64:(n + 1) * 64, 128:] + 0.9 * base)
        for unit, (a, b) in enumerate(owners):
            picks = picks_of(a, b)
            pack(s * 2 + unit, by_frequency(grid_b[2 * unit], grid_b[2 * unit + 1]), picks)
            keep(s * 2 + unit, by_frequency(grid_a[2 * unit], grid_a[2 * unit + 1]), picks)
        for unit, (a, b) in enumerate(owners):
            ship_own(s * 2 + unit, a, b)
        return carry

    lax.fori_loop(0, X - 1, pair_step, 0)

    for copy in swaps:
        copy.wait_recv()
    for half in range(2):
        half_copy(far, half, mate).wait_recv()
        half_copy(far, half, mate).start()
    high, low = encode([xt[half_rows(far, half), :] for half in range(2)])
    grid = mm(jnp.concatenate([high, low, high], axis=1), wx[...])
    bases = [own_base(far, half) for half in range(2)]
    picks = picks_of(far, far)
    pack(6, by_frequency(*[grid[n * 64:(n + 1) * 64, 128:256] + 0.9 * bases[n] for n in range(2)]), picks)
    ship_own(6, far, far)
    theirs = (mask_mate[...], pull_mate[...], [val_mate[:, k * 128:(k + 1) * 128] for k in range(BAND)])
    pack(8, by_frequency(*[grid[n * 64:(n + 1) * 64, 256:] + 0.9 * gm_mate[n * 64:(n + 1) * 64, :] for n in range(2)]), theirs)
    for i in range(Y):
        ship(8, far, i, mate).start()
    keep(6, by_frequency(*[grid[n * 64:(n + 1) * 64, :128] + 0.81 * bases[n] for n in range(2)]), picks)

    write_pair(X - 2)
    for half in range(2):
        half_copy(far_mate, half, mate).wait_recv()
    high, low = encode([xt[half_rows(far_mate, half), :] for half in range(2)])
    grid = mm(jnp.concatenate([high, low, high], axis=1), wx[:, 0:128])
    picks = picks_of(far_mate, far_mate)
    keep(7, by_frequency(*[grid[n * 64:(n + 1) * 64] + 0.81 * own_base(far_mate, n) for n in range(2)]), picks)
    write_pair(X - 1)

    for k in range(BAND):
        own[k] = val[pl.ds(pl.multiple_of(cz * 8, 8), 8), k * 128:(k + 1) * 128]
    own[BAND] = eight_of(push, cz)
    def wait_sums(count):
        some = recv.at[pl.ds(0, count)]
        pltpu.make_async_copy(some, some, sum_recv).wait()
        pltpu.make_async_copy(some, some, sum_send).wait()

    @pl.when(crossed)
    def _():
        wait_sums(GROUPS)

    @pl.when(jnp.logical_not(crossed))
    def _():
        wait_sums(GROUPS - 1)

    for copy in swaps:
        copy.wait_send()
    sent = xt.at[pl.ds(0, 7 * SHARD), :]
    pltpu.make_async_copy(sent, sent, gather_send).wait()


def finish(new_ref, recv, own, coldec, rowdec, out_hbm, upd_hbm, tot, upd, sem):
    cy = lax.axis_index("dp") % Y
    rows = ROWS // PARTS
    copies = [
        pltpu.make_async_copy(
            new_ref.at[0, pl.ds(n * rows, rows), :], out_hbm.at[0, pl.ds(n * rows, rows), :], sem.at[n]
        )
        for n in range(PARTS)
    ]
    for copy in copies:
        copy.start()
    tot[...] = jnp.zeros((32, 128), F32)
    tot[pl.ds(pl.multiple_of(cy * 8, 8), 8), :] = jnp.sum(recv[...], axis=0)
    behind = own[BAND]
    vals = [own[k] for k in range(BAND)]
    sums = []
    for part in range(2):
        for k in range(BAND // 2):
            packed = tot[pl.ds(k, 8, stride=4), :]
            if part:
                packed = pltpu.roll(packed, 128 - BAND, 1)
            full = jnp.zeros((8, 128), F32)
            for shift in range(9):
                moved = pltpu.roll(packed, shift, 1) if shift else packed
                full = jnp.where(behind == shift, moved, full)
            sums.append(full)
    kept = []
    for f in range(LOW):
        hit = jnp.zeros((8, 128), F32)
        for k in range(max(0, f - 8), min(7, f) + 1):
            hit = jnp.where(vals[k] == f, sums[k], hit)
        kept.append(hit)
    wide = widen(jnp.concatenate(kept, axis=0), coldec[...])
    high, low = split(wide)
    dec = rowdec[pl.ds(pl.multiple_of(cy * 128, 128), 128), :]
    upd[...] = mm(
        jnp.concatenate([dec[:, :128], dec], axis=1), jnp.concatenate([high, low, high], axis=0)
    )

    last = pltpu.make_async_copy(upd, upd_hbm, sem.at[PARTS])
    last.start()
    for copy in copies:
        copy.wait()
    last.wait()


def shards(inputs, out_grads, momentum, band):
    consts = [jnp.asarray(c) for c in constants()]
    band_t = jnp.transpose(band, (1, 2, 3, 0))
    hbm = pl.BlockSpec(memory_space=pltpu.HBM)
    vmem = pl.BlockSpec(memory_space=pltpu.VMEM)
    parts = pl.pallas_call(
        kernel,
        out_shape=(
            pltpu.VMEM(momentum.shape, BF16),
            pltpu.VMEM((GROUPS, 8, 128), F32),
            pltpu.VMEM((BAND + 1, 8, 128), F32),
            pltpu.VMEM((256, COLS), BF16),
            pltpu.VMEM((SHARD, 256), BF16),
        ),
        in_specs=[hbm] * 8,
        out_specs=(vmem,) * 5,
        scratch_shapes=[
            pltpu.VMEM((STEPS, TOK, SHARD), BF16),
            pltpu.VMEM((STEPS, TOK, COLS), BF16),
            pltpu.VMEM((ROWS, COLS), BF16),
            pltpu.VMEM((8, 2, 8, 64), jnp.int32),
            pltpu.VMEM((128, 256), F32),
            pltpu.VMEM((512, 256), F32),
            pltpu.VMEM((512, 256), F32),
            pltpu.VMEM((256, 512), F32),
            pltpu.VMEM((128, 256), BF16),
            pltpu.VMEM((512, 256), BF16),
            pltpu.VMEM((ROWS, STEPS * TOK), BF16),
            pltpu.VMEM((64, 2048), F32),
            pltpu.VMEM((64, 128), F32),
            pltpu.VMEM((64, 128), F32),
            pltpu.VMEM((64, 128), F32),
            pltpu.VMEM((768, 384), BF16),
            pltpu.VMEM((2, 768, COLS), BF16),
            pltpu.VMEM((X, 256, 128), F32),
            pltpu.VMEM((CHUNKS, 128, 128), F32),
            pltpu.VMEM((CHUNKS + 1, 32, 128), F32),
            pltpu.VMEM((128, 128), F32),
            pltpu.VMEM((8, 1024), F32),
            pltpu.VMEM((8, 128), F32),
            pltpu.VMEM((8, 128), F32),
            pltpu.SemaphoreType.DMA((8,)),
            pltpu.SemaphoreType.DMA((X,)),
            pltpu.SemaphoreType.DMA,
            pltpu.SemaphoreType.DMA((CHUNKS * 2,)),
            pltpu.SemaphoreType.DMA,
            pltpu.SemaphoreType.DMA,
            pltpu.SemaphoreType.DMA((5,)),
            pltpu.SemaphoreType.DMA((5,)),
        ],
        compiler_params=pltpu.CompilerParams(
            collective_id=0, has_side_effects=True, vmem_limit_bytes=40 * 1024 * 1024
        ),
        name="demo_steps",
    )(*[pltpu.with_memory_space_constraint(a, pltpu.HBM) for a in (inputs, out_grads, momentum, band_t, *consts)])
    parts = [pltpu.with_memory_space_constraint(a, pltpu.VMEM) for a in parts]
    return pl.pallas_call(
        finish,
        out_shape=(pltpu.HBM(momentum.shape, BF16), pltpu.HBM((128, COLS), F32)),
        in_specs=[vmem] * 5,
        out_specs=(hbm, hbm),
        scratch_shapes=[
            pltpu.VMEM((32, 128), F32),
            pltpu.VMEM((128, COLS), F32),
            pltpu.SemaphoreType.DMA((PARTS + 1,)),
        ],
        compiler_params=pltpu.CompilerParams(vmem_limit_bytes=8 * 1024 * 1024),
        name="demo_finish",
    )(*parts)


def solution(mesh):
    return jax.shard_map(
        shards,
        mesh=mesh,
        in_specs=(
            P(None, "dp", "tensor"),
            P(None, "dp", "tensor"),
            P("dp", None, "tensor"),
            P(None, "tensor", None, None),
        ),
        out_specs=(P("dp", None, "tensor"), P("dp", "tensor")),
        check_vma=False,
    )
```

```python
import functools
import math

import jax
import jax.numpy as jnp
import ml_dtypes
import numpy as np
from jax import lax
from jax.experimental import pallas as pl
from jax.experimental.pallas import tpu as pltpu
from jax.sharding import PartitionSpec as P

MESH = pl.DeviceIdType.MESH
F32 = jnp.float32
BF16 = jnp.bfloat16
SPAN = 64
LOW = 16
BAND = 8
TOK = 128
ROWS = 4096
COLS = 512
SHARD = 512
STEPS = 2
X = 4
GROUPS = 32
Y = 4
Z = 8
HALF = SHARD // 2
CHUNKS = 8
PARTS = 1
FACTOR = 1.0 / math.sqrt(TOK)


def split_const(table):
    high = table.astype(ml_dtypes.bfloat16).astype(np.float32)
    return high, (table - high).astype(ml_dtypes.bfloat16).astype(np.float32)


def low_rows():
    freq = np.arange(LOW)[:, None]
    place = np.arange(SPAN)[None, :]
    table = np.sqrt(2.0 / SPAN) * np.cos(math.pi * (2.0 * place + 1.0) * freq / (2.0 * SPAN))
    table[0] /= math.sqrt(2.0)
    return table.astype(np.float32)


def constants():
    low = low_rows()
    four = np.zeros((LOW, 4, 4, SPAN), np.float32)
    enc = np.zeros((LOW, 8, 8, SPAN), np.float32)
    col = np.zeros((8, SPAN, 8, LOW), np.float32)
    for block in range(8):
        enc[:, block, block, :] = low
        col[block, :, block, :] = low.T
        if block < 4:
            four[:, block, block, :] = low
    rowenc = np.concatenate(split_const(four.reshape(64, 256)), axis=0)
    rowdec = np.concatenate(split_const(enc.reshape(128, 512).T), axis=1)
    colenc = np.concatenate(split_const(col.reshape(512, 128)), axis=1)
    high, lower = split_const(col.reshape(512, 128).T)
    zero = np.zeros((64, 256), np.float32)
    first = [high[:64, :256], lower[:64, :256], high[:64, :256], zero]
    second = [lower[64:, 256:], high[64:, 256:], zero, high[64:, 256:]]
    coldec = np.concatenate([np.concatenate(first, axis=0), np.concatenate(second, axis=0)], axis=1)
    return rowenc, rowdec, colenc, coldec


def split(a):
    high = a.astype(BF16)
    low = (a - high.astype(F32)).astype(BF16)
    return high, low


def mm(a, b):
    return jnp.dot(a, b, preferred_element_type=F32)


def widen(grids, coldec):
    lane = lax.broadcasted_iota(jnp.int32, grids.shape, 1) < 64
    turned = pltpu.roll(grids, 64, 1)
    high, low = split(grids)
    first = jnp.concatenate([jnp.where(lane, grids, turned).astype(BF16), low], axis=1)
    second = jnp.concatenate([jnp.where(lane, turned, grids).astype(BF16), low], axis=1)
    return jnp.concatenate([mm(first, coldec[:, :256]), mm(second, coldec[:, 256:])], axis=1)


def kernel(
    x_hbm, d_hbm, m_hbm, band_hbm, rowenc_hbm, rowdec_hbm, colenc_hbm, coldec_hbm,
    out_ref, recv, own, coldec, rowdec,
    xin, din, m_ref, band_ref, rowenc_in, rowdec_in, colenc_in, coldec_in, rowenc, colenc,
    xt, val, colmask, pull, push, wx, rhs, gm, kept, send, gm_mate, val_mate, pull_mate, mask_mate,
    load_sem, m_sem, gather_send, gather_recv, sum_send, sum_recv, swap_send, swap_recv,
    z_token, y_token, mate_token,
):
    dp = lax.axis_index("dp")
    tensor = lax.axis_index("tensor")
    cx = tensor // 2
    core = tensor % 2
    cz = dp // Y
    cy = dp % Y

    def tensor_of(hop, other):
        return 2 * ((cx + hop) % X) + (core + other) % 2

    mate = tensor_of(0, 1)
    right = tensor_of(1, 0)
    left = tensor_of(X - 1, 0)
    far = tensor_of(2, 0)
    far_mate = tensor_of(2, 1)
    crossed = cz == far_mate

    def load(src, dst, n):
        copy = pltpu.make_async_copy(src, dst, load_sem.at[n])
        copy.start()
        return copy

    x_loads = [
        load(x_hbm.at[:, :, half * 256:(half + 1) * 256], xin.at[:, :, half * 256:(half + 1) * 256], half)
        for half in range(2)
    ]
    def column(dz, dy):
        return (cz + dz) % Z * Y + (cy + dy) % Y

    z_far = [column(2, 0), column(Z - 2, 0)]
    y_peers = [column(0, n) for n in range(1, Y)]
    near = [(dp, mate), (dp, right), (dp, left)]
    near += [(peer, tensor) for peer in (column(1, 0), column(Z - 1, 0), *z_far, *y_peers)]
    barrier = pltpu.get_barrier_semaphore()
    for peer in near:
        pl.semaphore_signal(barrier, inc=1, device_id=peer, device_id_type=MESH)
    colenc_load = load(colenc_hbm, colenc_in, 2)
    d_load = load(d_hbm, din, 3)
    band_load = load(band_hbm, band_ref, 4)
    rowenc_load = load(rowenc_hbm, rowenc_in, 5)
    coldec_load = load(coldec_hbm, coldec_in, 6)
    rowdec_load = load(rowdec_hbm, rowdec_in, 7)

    def m_copy(p):
        rows = pl.ds(pl.multiple_of(p * 2 * SHARD, 2 * SHARD), 2 * SHARD)
        return pltpu.make_async_copy(m_hbm.at[0, rows, :], m_ref.at[rows, :], m_sem.at[p])

    for p in range(X):
        m_copy(p).start()

    def half_copy(owner, half, target):
        rows = pl.ds(pl.multiple_of(owner * SHARD + half * HALF, HALF), HALF)
        return pltpu.make_async_remote_copy(
            src_ref=xt.at[rows, :],
            dst_ref=xt.at[rows, :],
            send_sem=gather_send,
            recv_sem=gather_recv.at[owner * 2 + half],
            device_id=(dp, target),
            device_id_type=MESH,
        )

    def turn(half):
        x_loads[half].wait()
        rows = pl.ds(pl.multiple_of(tensor * SHARD + half * HALF, HALF), HALF)
        for step in range(STEPS):
            xt[rows, step * TOK:(step + 1) * TOK] = xin[step, :, half * HALF:(half + 1) * HALF].T

    turn(0)
    pl.semaphore_wait(barrier, len(near))
    half_copy(tensor, 0, right).start()
    turn(1)
    half_copy(tensor, 1, left).start()
    half_copy(tensor, 0, mate).start()
    half_copy(tensor, 1, mate).start()
    half_copy(tensor, 1, right).start()
    half_copy(tensor, 0, left).start()

    for peer in z_far:
        pl.semaphore_signal(z_token, inc=1, device_id=(peer, tensor), device_id_type=MESH)

    colenc_load.wait()
    colenc[...] = colenc_in[...].astype(BF16)
    d_load.wait()
    both = mm(jnp.concatenate([din[0], din[1]], axis=0), colenc[...])
    hats = (both[:, :128] + both[:, 128:]) * FACTOR
    table = jnp.concatenate(
        [jnp.concatenate([0.9 * hats[:128], hats[:128]], axis=1), jnp.concatenate([hats[128:], hats[128:]], axis=1)],
        axis=0,
    )
    high, low = split(table)
    wx[0:256, 0:256] = high
    wx[256:512, 0:256] = high
    wx[512:768, 0:256] = low
    high, low = split(0.9 * din[0].astype(F32))
    for unit in range(2):
        rhs[unit, 0:128, :] = high
        rhs[unit, 128:256, :] = din[1]
        rhs[unit, 256:384, :] = low

    band_load.wait()
    picks = band_ref[...].reshape(128, 64).astype(F32).T.astype(BF16)
    away = lax.broadcasted_iota(jnp.int32, (128, 128), 0) - lax.broadcasted_iota(jnp.int32, (128, 128), 1) // LOW * 16
    for n in range(2 * BAND):
        val[:, n * 128:(n + 1) * 128] = mm(picks, (away == n).astype(F32).astype(BF16))
    place = (lax.broadcasted_iota(jnp.int32, (64, 128), 1) % LOW).astype(F32)
    seen = jnp.zeros((64, 128), F32)
    ahead = jnp.zeros((64, 128), F32)
    back = jnp.full((64, 128), -1.0, F32)
    for k in range(BAND):
        freq = val[:, (BAND + k) * 128:(BAND + k + 1) * 128]
        seen = jnp.where(freq == place, 1.0, seen)
        back = jnp.where(freq == place, place - k, back)
        ahead = jnp.where(place == k, freq - k, ahead)
    colmask[...] = seen
    pull[...] = ahead
    push[...] = back

    rowenc_load.wait()
    rowenc[...] = rowenc_in[...].astype(BF16)

    def encode(halves):
        wide = mm(rowenc[...], jnp.concatenate(halves, axis=1))
        wide = wide[:64] + wide[64:]
        size = halves[0].shape[1]
        return split(jnp.concatenate([wide[:, n * size:(n + 1) * size] for n in range(len(halves))], axis=0))

    def momentum_step(p, carry):
        m_copy(p).wait()
        high, low = encode(
            [m_ref[pl.ds(pl.multiple_of(p * 2 * SHARD + n * HALF, HALF), HALF), :] for n in range(4)]
        )
        both = mm(jnp.concatenate([high, low], axis=0), colenc[...])
        gm[p] = both[:256, :128] + both[:256, 128:] + both[256:, :128]
        return carry

    pl.semaphore_wait(z_token, 2)
    for peer in y_peers:
        pl.semaphore_signal(y_token, inc=1, device_id=(peer, tensor), device_id_type=MESH)

    lax.fori_loop(0, X, momentum_step, 0)

    pl.semaphore_wait(y_token, Y - 1)
    pl.semaphore_signal(mate_token, inc=1, device_id=(dp, mate), device_id_type=MESH)

    def swap(src, dst, n):
        return pltpu.make_async_remote_copy(
            src_ref=src, dst_ref=dst, send_sem=swap_send.at[n], recv_sem=swap_recv.at[n],
            device_id=(dp, mate), device_id_type=MESH,
        )

    mate_rows = pl.ds(pl.multiple_of(far_mate * 8, 8), 8)
    swaps = [
        swap(wx.at[:, 128:256], wx.at[:, 256:384], 0),
        swap(gm.at[far_mate // 2, pl.ds(pl.multiple_of(far_mate % 2 * 128, 128), 128), :], gm_mate, 1),
        swap(val.at[mate_rows, 0:1024], val_mate, 2),
        swap(pull.at[mate_rows, :], pull_mate, 3),
        swap(colmask.at[mate_rows, :], mask_mate, 4),
    ]
    for copy in swaps:
        copy.start()
    coldec_load.wait()
    coldec[...] = coldec_in[...].astype(BF16)
    rowdec_load.wait()
    rowdec[...] = rowdec_in[...].astype(BF16)

    top = lax.broadcasted_iota(jnp.int32, (8, 128), 0) < 4
    lane = lax.broadcasted_iota(jnp.int32, (8, 128), 1) % LOW < BAND

    def eight_of(ref, owner):
        return ref[pl.ds(pl.multiple_of(owner * 8, 8), 8), :]

    def owners_of(s):
        hop_a = jnp.where(s == 0, 0, jnp.where(s == 1, X - 1, jnp.where(s == 2, 1, 2)))
        hop_b = jnp.where(s == 0, 0, jnp.where(s == 1, 1, jnp.where(s == 2, X - 1, 2)))
        return [(tensor_of(hop_a, other), tensor_of(hop_b, other)) for other in range(2)]

    def half_rows(owner, half):
        return pl.ds(pl.multiple_of(owner * SHARD + half * HALF, HALF), HALF)

    def write_pair(s):
        grids = jnp.concatenate([kept[s * 2], kept[s * 2 + 1]], axis=0)
        wide = widen(grids, coldec[...]) * (-1.0 / FACTOR)
        high, low = split(wide)
        for unit, (a, b) in enumerate(owners_of(s)):
            here = slice(unit * 128, (unit + 1) * 128)
            rhs[unit, 384:512, :] = high[here]
            rhs[unit, 512:640, :] = low[here]
            rhs[unit, 640:768, :] = high[here]
        for unit, (a, b) in enumerate(owners_of(s)):
            for half, owner in enumerate((a, b)):
                rows = half_rows(owner, half)
                part = xt[rows, :]
                dec = rowdec[half * HALF:(half + 1) * HALF, :]
                left_side = jnp.concatenate([part, part[:, :128], dec[:, :128], dec], axis=1)
                change = mm(left_side, rhs[unit])
                out_ref[0, rows, :] = (0.81 * m_ref[rows, :].astype(F32) + FACTOR * change).astype(BF16)

    def by_frequency(first, second):
        tiles = []
        for n in range(LOW // 2):
            one, two = first[8 * n:8 * n + 8], second[8 * n:8 * n + 8]
            tiles.append(jnp.where(top, one, pltpu.roll(two, 4, 0)))
            tiles.append(jnp.where(top, pltpu.roll(one, 4, 0), two))
        return tiles

    def picks_of(a, b):
        def mixed(ref, cols=slice(0, 128)):
            rows_a = pl.ds(pl.multiple_of(a * 8, 8), 8)
            rows_b = pl.ds(pl.multiple_of(b * 8, 8), 8)
            return jnp.where(top, ref[rows_a, cols], ref[rows_b, cols])

        return mixed(colmask), mixed(pull), [mixed(val, slice(k * 128, (k + 1) * 128)) for k in range(BAND)]

    def pack(stage, tiles, picks):
        mask, ahead, vals = picks
        thin = []
        for k in range(BAND):
            got = tiles[k]
            for f in range(k + 1, k + 9):
                got = jnp.where(vals[k] == f, tiles[f], got)
            moved = got
            for shift in range(1, 9):
                moved = jnp.where(ahead == shift, pltpu.roll(got, 128 - shift, 1), moved)
            thin.append(moved)
        for k in range(BAND // 2):
            packed = jnp.where(lane, thin[k], pltpu.roll(thin[k + BAND // 2], BAND, 1))
            send[stage, pl.ds(k, 8, stride=4), :] = packed

    def keep(unit, tiles, picks):
        mask, ahead, vals = picks
        for f in range(LOW):
            hit = jnp.zeros((8, 128), F32)
            for k in range(max(0, f - 8), min(7, f) + 1):
                hit = jnp.where(vals[k] == f, mask, hit)
            kept[unit, 8 * f:8 * f + 8, :] = hit * tiles[f]

    def own_base(owner, half):
        start = pl.multiple_of((owner % 2) * 128 + half * 64, 64)
        return gm[owner // 2, pl.ds(start, 64), :]

    def ship(stage, owner, i, column):
        return pltpu.make_async_remote_copy(
            src_ref=send.at[stage, pl.ds(i * 8, 8), :],
            dst_ref=recv.at[dp],
            send_sem=sum_send,
            recv_sem=sum_recv,
            device_id=(owner * Y + i, column),
            device_id_type=MESH,
        )

    def ship_own(stage, a, b):
        for i in range(Y):
            owner = a if i < Y // 2 else b

            @pl.when(owner * Y + i != dp)
            def _():
                ship(stage, owner, i, tensor).start()

            @pl.when(owner * Y + i == dp)
            def _():
                recv[dp] = send[stage, i * 8:(i + 1) * 8, :]

    def pair_step(s, carry):
        owners = owners_of(s)

        @pl.when(s > 0)
        def _():
            half_copy(owners[0][0], 0, mate).wait_recv()
            half_copy(owners[0][0], 0, mate).start()

            @pl.when(s == 1)
            def _():
                half_copy(left, 0, right).start()

            half_copy(owners[0][1], 1, mate).wait_recv()
            half_copy(owners[0][1], 1, mate).start()

            @pl.when(s == 1)
            def _():
                half_copy(right, 1, left).start()

            write_pair(s - 1)

        half_copy(owners[1][0], 0, mate).wait_recv()
        half_copy(owners[1][1], 1, mate).wait_recv()

        quarters = [(a, 0) if half == 0 else (b, 1) for a, b in owners for half in range(2)]
        high, low = encode([xt[half_rows(owner, half), :] for owner, half in quarters])
        grid = mm(jnp.concatenate([high, low, high], axis=1), wx[:, 0:256])
        grid_a, grid_b = [], []
        for n, (owner, half) in enumerate(quarters):
            base = own_base(owner, half)
            grid_a.append(grid[n * 64:(n + 1) * 64, :128] + 0.81 * base)
            grid_b.append(grid[n * 64:(n + 1) * 64, 128:] + 0.9 * base)
        for unit, (a, b) in enumerate(owners):
            picks = picks_of(a, b)
            pack(s * 2 + unit, by_frequency(grid_b[2 * unit], grid_b[2 * unit + 1]), picks)
            keep(s * 2 + unit, by_frequency(grid_a[2 * unit], grid_a[2 * unit + 1]), picks)
        for unit, (a, b) in enumerate(owners):
            ship_own(s * 2 + unit, a, b)
        return carry

    lax.fori_loop(0, X - 1, pair_step, 0)

    pl.semaphore_wait(mate_token, 1)
    for copy in swaps:
        copy.wait_recv()
    for half in range(2):
        half_copy(far, half, mate).wait_recv()
        half_copy(far, half, mate).start()
    high, low = encode([xt[half_rows(far, half), :] for half in range(2)])
    grid = mm(jnp.concatenate([high, low, high], axis=1), wx[...])
    bases = [own_base(far, half) for half in range(2)]
    picks = picks_of(far, far)
    pack(6, by_frequency(*[grid[n * 64:(n + 1) * 64, 128:256] + 0.9 * bases[n] for n in range(2)]), picks)
    ship_own(6, far, far)
    theirs = (mask_mate[...], pull_mate[...], [val_mate[:, k * 128:(k + 1) * 128] for k in range(BAND)])
    pack(8, by_frequency(*[grid[n * 64:(n + 1) * 64, 256:] + 0.9 * gm_mate[n * 64:(n + 1) * 64, :] for n in range(2)]), theirs)
    for i in range(Y):
        ship(8, far, i, mate).start()
    keep(6, by_frequency(*[grid[n * 64:(n + 1) * 64, :128] + 0.81 * bases[n] for n in range(2)]), picks)

    write_pair(X - 2)
    for half in range(2):
        half_copy(far_mate, half, mate).wait_recv()
    high, low = encode([xt[half_rows(far_mate, half), :] for half in range(2)])
    grid = mm(jnp.concatenate([high, low, high], axis=1), wx[:, 0:128])
    picks = picks_of(far_mate, far_mate)
    keep(7, by_frequency(*[grid[n * 64:(n + 1) * 64] + 0.81 * own_base(far_mate, n) for n in range(2)]), picks)
    write_pair(X - 1)

    for k in range(BAND):
        own[k] = val[pl.ds(pl.multiple_of(cz * 8, 8), 8), k * 128:(k + 1) * 128]
    own[BAND] = eight_of(push, cz)
    def wait_sums(count):
        some = recv.at[pl.ds(0, count)]
        pltpu.make_async_copy(some, some, sum_recv).wait()
        pltpu.make_async_copy(some, some, sum_send).wait()

    @pl.when(crossed)
    def _():
        wait_sums(GROUPS)

    @pl.when(jnp.logical_not(crossed))
    def _():
        wait_sums(GROUPS - 1)

    for copy in swaps:
        copy.wait_send()
    sent = xt.at[pl.ds(0, 7 * SHARD), :]
    pltpu.make_async_copy(sent, sent, gather_send).wait()


def finish(new_ref, recv, own, coldec, rowdec, out_hbm, upd_hbm, tot, upd, sem):
    cy = lax.axis_index("dp") % Y
    rows = ROWS // PARTS
    copies = [
        pltpu.make_async_copy(
            new_ref.at[0, pl.ds(n * rows, rows), :], out_hbm.at[0, pl.ds(n * rows, rows), :], sem.at[n]
        )
        for n in range(PARTS)
    ]
    for copy in copies:
        copy.start()
    tot[...] = jnp.zeros((32, 128), F32)
    tot[pl.ds(pl.multiple_of(cy * 8, 8), 8), :] = jnp.sum(recv[...], axis=0)
    behind = own[BAND]
    vals = [own[k] for k in range(BAND)]
    sums = []
    for part in range(2):
        for k in range(BAND // 2):
            packed = tot[pl.ds(k, 8, stride=4), :]
            if part:
                packed = pltpu.roll(packed, 128 - BAND, 1)
            full = jnp.zeros((8, 128), F32)
            for shift in range(9):
                moved = pltpu.roll(packed, shift, 1) if shift else packed
                full = jnp.where(behind == shift, moved, full)
            sums.append(full)
    kept = []
    for f in range(LOW):
        hit = jnp.zeros((8, 128), F32)
        for k in range(max(0, f - 8), min(7, f) + 1):
            hit = jnp.where(vals[k] == f, sums[k], hit)
        kept.append(hit)
    wide = widen(jnp.concatenate(kept, axis=0), coldec[...])
    high, low = split(wide)
    dec = rowdec[pl.ds(pl.multiple_of(cy * 128, 128), 128), :]
    upd[...] = mm(
        jnp.concatenate([dec[:, :128], dec], axis=1), jnp.concatenate([high, low, high], axis=0)
    )

    last = pltpu.make_async_copy(upd, upd_hbm, sem.at[PARTS])
    last.start()
    for copy in copies:
        copy.wait()
    last.wait()


def shards(inputs, out_grads, momentum, band):
    consts = [jnp.asarray(c) for c in constants()]
    band_t = jnp.transpose(band, (1, 2, 3, 0))
    hbm = pl.BlockSpec(memory_space=pltpu.HBM)
    vmem = pl.BlockSpec(memory_space=pltpu.VMEM)
    parts = pl.pallas_call(
        kernel,
        out_shape=(
            pltpu.VMEM(momentum.shape, BF16),
            pltpu.VMEM((GROUPS, 8, 128), F32),
            pltpu.VMEM((BAND + 1, 8, 128), F32),
            pltpu.VMEM((256, COLS), BF16),
            pltpu.VMEM((SHARD, 256), BF16),
        ),
        in_specs=[hbm] * 8,
        out_specs=(vmem,) * 5,
        scratch_shapes=[
            pltpu.VMEM((STEPS, TOK, SHARD), BF16),
            pltpu.VMEM((STEPS, TOK, COLS), BF16),
            pltpu.VMEM((ROWS, COLS), BF16),
            pltpu.VMEM((8, 2, 8, 64), jnp.int32),
            pltpu.VMEM((128, 256), F32),
            pltpu.VMEM((512, 256), F32),
            pltpu.VMEM((512, 256), F32),
            pltpu.VMEM((256, 512), F32),
            pltpu.VMEM((128, 256), BF16),
            pltpu.VMEM((512, 256), BF16),
            pltpu.VMEM((ROWS, STEPS * TOK), BF16),
            pltpu.VMEM((64, 2048), F32),
            pltpu.VMEM((64, 128), F32),
            pltpu.VMEM((64, 128), F32),
            pltpu.VMEM((64, 128), F32),
            pltpu.VMEM((768, 384), BF16),
            pltpu.VMEM((2, 768, COLS), BF16),
            pltpu.VMEM((X, 256, 128), F32),
            pltpu.VMEM((CHUNKS, 128, 128), F32),
            pltpu.VMEM((CHUNKS + 1, 32, 128), F32),
            pltpu.VMEM((128, 128), F32),
            pltpu.VMEM((8, 1024), F32),
            pltpu.VMEM((8, 128), F32),
            pltpu.VMEM((8, 128), F32),
            pltpu.SemaphoreType.DMA((8,)),
            pltpu.SemaphoreType.DMA((X,)),
            pltpu.SemaphoreType.DMA,
            pltpu.SemaphoreType.DMA((CHUNKS * 2,)),
            pltpu.SemaphoreType.DMA,
            pltpu.SemaphoreType.DMA,
            pltpu.SemaphoreType.DMA((5,)),
            pltpu.SemaphoreType.DMA((5,)),
            pltpu.SemaphoreType.REGULAR,
            pltpu.SemaphoreType.REGULAR,
            pltpu.SemaphoreType.REGULAR,
        ],
        compiler_params=pltpu.CompilerParams(
            collective_id=0, has_side_effects=True, vmem_limit_bytes=40 * 1024 * 1024
        ),
        name="demo_steps",
    )(*[pltpu.with_memory_space_constraint(a, pltpu.HBM) for a in (inputs, out_grads, momentum, band_t, *consts)])
    parts = [pltpu.with_memory_space_constraint(a, pltpu.VMEM) for a in parts]
    return pl.pallas_call(
        finish,
        out_shape=(pltpu.HBM(momentum.shape, BF16), pltpu.HBM((128, COLS), F32)),
        in_specs=[vmem] * 5,
        out_specs=(hbm, hbm),
        scratch_shapes=[
            pltpu.VMEM((32, 128), F32),
            pltpu.VMEM((128, COLS), F32),
            pltpu.SemaphoreType.DMA((PARTS + 1,)),
        ],
        compiler_params=pltpu.CompilerParams(vmem_limit_bytes=8 * 1024 * 1024),
        name="demo_finish",
    )(*parts)


def solution(mesh):
    return jax.shard_map(
        shards,
        mesh=mesh,
        in_specs=(
            P(None, "dp", "tensor"),
            P(None, "dp", "tensor"),
            P("dp", None, "tensor"),
            P(None, "tensor", None, None),
        ),
        out_specs=(P("dp", None, "tensor"), P("dp", "tensor")),
        check_vma=False,
    )
```

```python
import functools
import math

import jax
import jax.numpy as jnp
import ml_dtypes
import numpy as np
from jax import lax
from jax.experimental import pallas as pl
from jax.experimental.pallas import tpu as pltpu
from jax.sharding import PartitionSpec as P

MESH = pl.DeviceIdType.MESH
F32 = jnp.float32
BF16 = jnp.bfloat16
SPAN = 64
LOW = 16
BAND = 8
TOK = 128
ROWS = 4096
COLS = 512
SHARD = 512
STEPS = 2
X = 4
GROUPS = 32
Y = 4
Z = 8
HALF = SHARD // 2
CHUNKS = 8
PARTS = 1
FACTOR = 1.0 / math.sqrt(TOK)


def split_const(table):
    high = table.astype(ml_dtypes.bfloat16).astype(np.float32)
    return high, (table - high).astype(ml_dtypes.bfloat16).astype(np.float32)


def low_rows():
    freq = np.arange(LOW)[:, None]
    place = np.arange(SPAN)[None, :]
    table = np.sqrt(2.0 / SPAN) * np.cos(math.pi * (2.0 * place + 1.0) * freq / (2.0 * SPAN))
    table[0] /= math.sqrt(2.0)
    return table.astype(np.float32)


def constants():
    low = low_rows()
    four = np.zeros((LOW, 4, 4, SPAN), np.float32)
    enc = np.zeros((LOW, 8, 8, SPAN), np.float32)
    col = np.zeros((8, SPAN, 8, LOW), np.float32)
    for block in range(8):
        enc[:, block, block, :] = low
        col[block, :, block, :] = low.T
        if block < 4:
            four[:, block, block, :] = low
    rowenc = np.concatenate(split_const(four.reshape(64, 256)), axis=0)
    rowdec = np.concatenate(split_const(enc.reshape(128, 512).T), axis=1)
    colenc = np.concatenate(split_const(col.reshape(512, 128)), axis=1)
    high, lower = split_const(col.reshape(512, 128).T)
    zero = np.zeros((64, 256), np.float32)
    first = [high[:64, :256], lower[:64, :256], high[:64, :256], zero]
    second = [lower[64:, 256:], high[64:, 256:], zero, high[64:, 256:]]
    coldec = np.concatenate([np.concatenate(first, axis=0), np.concatenate(second, axis=0)], axis=1)
    return rowenc, rowdec, colenc, coldec


def split(a):
    high = a.astype(BF16)
    low = (a - high.astype(F32)).astype(BF16)
    return high, low


def mm(a, b):
    return jnp.dot(a, b, preferred_element_type=F32)


def widen(grids, coldec):
    lane = lax.broadcasted_iota(jnp.int32, grids.shape, 1) < 64
    turned = pltpu.roll(grids, 64, 1)
    high, low = split(grids)
    first = jnp.concatenate([jnp.where(lane, grids, turned).astype(BF16), low], axis=1)
    second = jnp.concatenate([jnp.where(lane, turned, grids).astype(BF16), low], axis=1)
    return jnp.concatenate([mm(first, coldec[:, :256]), mm(second, coldec[:, 256:])], axis=1)


def kernel(
    x_hbm, d_hbm, m_hbm, band_hbm, rowenc_hbm, rowdec_hbm, colenc_hbm, coldec_hbm,
    out_ref, recv, own, coldec, rowdec,
    xin, din, m_ref, band_ref, rowenc_in, rowdec_in, colenc_in, coldec_in, rowenc, colenc,
    xt, val, colmask, pull, push, wx, rhs, gm, kept, send, gm_mate, val_mate, pull_mate, mask_mate,
    load_sem, m_sem, gather_send, gather_recv, sum_send, sum_recv, swap_send, swap_recv,
    z_token, y_token, mate_token,
):
    dp = lax.axis_index("dp")
    tensor = lax.axis_index("tensor")
    cx = tensor // 2
    core = tensor % 2
    cz = dp // Y
    cy = dp % Y

    def tensor_of(hop, other):
        return 2 * ((cx + hop) % X) + (core + other) % 2

    mate = tensor_of(0, 1)
    right = tensor_of(1, 0)
    left = tensor_of(X - 1, 0)
    far = tensor_of(2, 0)
    far_mate = tensor_of(2, 1)
    crossed = cz == far_mate

    def load(src, dst, n):
        copy = pltpu.make_async_copy(src, dst, load_sem.at[n])
        copy.start()
        return copy

    x_loads = [
        load(x_hbm.at[:, :, half * 256:(half + 1) * 256], xin.at[:, :, half * 256:(half + 1) * 256], half)
        for half in range(2)
    ]
    def column(dz, dy):
        return (cz + dz) % Z * Y + (cy + dy) % Y

    z_far = [column(2, 0), column(Z - 2, 0)]
    y_peers = [column(0, n) for n in range(1, Y)]
    near = [(dp, mate), (dp, right), (dp, left)]
    near += [(peer, tensor) for peer in (column(1, 0), column(Z - 1, 0), *z_far, *y_peers)]
    barrier = pltpu.get_barrier_semaphore()
    for peer in near:
        pl.semaphore_signal(barrier, inc=1, device_id=peer, device_id_type=MESH)
    colenc_load = load(colenc_hbm, colenc_in, 2)
    d_load = load(d_hbm, din, 3)
    band_load = load(band_hbm, band_ref, 4)
    rowenc_load = load(rowenc_hbm, rowenc_in, 5)
    coldec_load = load(coldec_hbm, coldec_in, 6)
    rowdec_load = load(rowdec_hbm, rowdec_in, 7)

    def m_copy(p):
        rows = pl.ds(pl.multiple_of(p * 2 * SHARD, 2 * SHARD), 2 * SHARD)
        return pltpu.make_async_copy(m_hbm.at[0, rows, :], m_ref.at[rows, :], m_sem.at[p])

    for p in range(X):
        m_copy(p).start()

    def half_copy(owner, half, target):
        rows = pl.ds(pl.multiple_of(owner * SHARD + half * HALF, HALF), HALF)
        return pltpu.make_async_remote_copy(
            src_ref=xt.at[rows, :],
            dst_ref=xt.at[rows, :],
            send_sem=gather_send,
            recv_sem=gather_recv.at[owner * 2 + half],
            device_id=(dp, target),
            device_id_type=MESH,
        )

    def turn(half):
        x_loads[half].wait()
        rows = pl.ds(pl.multiple_of(tensor * SHARD + half * HALF, HALF), HALF)
        for step in range(STEPS):
            xt[rows, step * TOK:(step + 1) * TOK] = xin[step, :, half * HALF:(half + 1) * HALF].T

    turn(0)
    pl.semaphore_wait(barrier, len(near))
    half_copy(tensor, 0, right).start()
    turn(1)
    half_copy(tensor, 1, left).start()
    half_copy(tensor, 0, mate).start()
    half_copy(tensor, 1, mate).start()
    half_copy(tensor, 1, right).start()
    half_copy(tensor, 0, left).start()

    for peer in z_far:
        pl.semaphore_signal(z_token, inc=1, device_id=(peer, tensor), device_id_type=MESH)

    colenc_load.wait()
    colenc[...] = colenc_in[...].astype(BF16)
    d_load.wait()
    both = mm(jnp.concatenate([din[0], din[1]], axis=0), colenc[...])
    hats = (both[:, :128] + both[:, 128:]) * FACTOR
    table = jnp.concatenate(
        [jnp.concatenate([0.9 * hats[:128], hats[:128]], axis=1), jnp.concatenate([hats[128:], hats[128:]], axis=1)],
        axis=0,
    )
    high, low = split(table)
    wx[0:256, 0:256] = high
    wx[256:512, 0:256] = high
    wx[512:768, 0:256] = low
    high, low = split(0.9 * din[0].astype(F32))
    for unit in range(2):
        rhs[unit, 0:128, :] = high
        rhs[unit, 128:256, :] = din[1]
        rhs[unit, 256:384, :] = low

    band_load.wait()
    picks = band_ref[...].reshape(128, 64).astype(F32).T.astype(BF16)
    away = lax.broadcasted_iota(jnp.int32, (128, 128), 0) - lax.broadcasted_iota(jnp.int32, (128, 128), 1) // LOW * 16
    for n in range(2 * BAND):
        val[:, n * 128:(n + 1) * 128] = mm(picks, (away == n).astype(F32).astype(BF16))
    place = (lax.broadcasted_iota(jnp.int32, (64, 128), 1) % LOW).astype(F32)
    seen = jnp.zeros((64, 128), F32)
    ahead = jnp.zeros((64, 128), F32)
    back = jnp.full((64, 128), -1.0, F32)
    for k in range(BAND):
        freq = val[:, (BAND + k) * 128:(BAND + k + 1) * 128]
        seen = jnp.where(freq == place, 1.0, seen)
        back = jnp.where(freq == place, place - k, back)
        ahead = jnp.where(place == k, freq - k, ahead)
    colmask[...] = seen
    pull[...] = ahead
    push[...] = back

    rowenc_load.wait()
    rowenc[...] = rowenc_in[...].astype(BF16)

    def encode(halves):
        wide = mm(rowenc[...], jnp.concatenate(halves, axis=1))
        wide = wide[:64] + wide[64:]
        size = halves[0].shape[1]
        return split(jnp.concatenate([wide[:, n * size:(n + 1) * size] for n in range(len(halves))], axis=0))

    def momentum_step(p, carry):
        m_copy(p).wait()
        high, low = encode(
            [m_ref[pl.ds(pl.multiple_of(p * 2 * SHARD + n * HALF, HALF), HALF), :] for n in range(4)]
        )
        both = mm(jnp.concatenate([high, low], axis=0), colenc[...])
        gm[p] = both[:256, :128] + both[:256, 128:] + both[256:, :128]
        return carry

    lax.fori_loop(0, X, momentum_step, 0)

    pl.semaphore_wait(z_token, 2)
    for peer in y_peers:
        pl.semaphore_signal(y_token, inc=1, device_id=(peer, tensor), device_id_type=MESH)

    def swap(src, dst, n):
        return pltpu.make_async_remote_copy(
            src_ref=src, dst_ref=dst, send_sem=swap_send.at[n], recv_sem=swap_recv.at[n],
            device_id=(dp, mate), device_id_type=MESH,
        )

    mate_rows = pl.ds(pl.multiple_of(far_mate * 8, 8), 8)
    swaps = [
        swap(wx.at[:, 128:256], wx.at[:, 256:384], 0),
        swap(gm.at[far_mate // 2, pl.ds(pl.multiple_of(far_mate % 2 * 128, 128), 128), :], gm_mate, 1),
        swap(val.at[mate_rows, 0:1024], val_mate, 2),
        swap(pull.at[mate_rows, :], pull_mate, 3),
        swap(colmask.at[mate_rows, :], mask_mate, 4),
    ]
    for copy in swaps:
        copy.start()
    coldec_load.wait()
    coldec[...] = coldec_in[...].astype(BF16)
    rowdec_load.wait()
    rowdec[...] = rowdec_in[...].astype(BF16)

    top = lax.broadcasted_iota(jnp.int32, (8, 128), 0) < 4
    lane = lax.broadcasted_iota(jnp.int32, (8, 128), 1) % LOW < BAND

    def eight_of(ref, owner):
        return ref[pl.ds(pl.multiple_of(owner * 8, 8), 8), :]

    def owners_of(s):
        hop_a = jnp.where(s == 0, 0, jnp.where(s == 1, X - 1, jnp.where(s == 2, 1, 2)))
        hop_b = jnp.where(s == 0, 0, jnp.where(s == 1, 1, jnp.where(s == 2, X - 1, 2)))
        return [(tensor_of(hop_a, other), tensor_of(hop_b, other)) for other in range(2)]

    def half_rows(owner, half):
        return pl.ds(pl.multiple_of(owner * SHARD + half * HALF, HALF), HALF)

    def write_pair(s):
        grids = jnp.concatenate([kept[s * 2], kept[s * 2 + 1]], axis=0)
        wide = widen(grids, coldec[...]) * (-1.0 / FACTOR)
        high, low = split(wide)
        for unit, (a, b) in enumerate(owners_of(s)):
            here = slice(unit * 128, (unit + 1) * 128)
            rhs[unit, 384:512, :] = high[here]
            rhs[unit, 512:640, :] = low[here]
            rhs[unit, 640:768, :] = high[here]
        for unit, (a, b) in enumerate(owners_of(s)):
            for half, owner in enumerate((a, b)):
                rows = half_rows(owner, half)
                part = xt[rows, :]
                dec = rowdec[half * HALF:(half + 1) * HALF, :]
                left_side = jnp.concatenate([part, part[:, :128], dec[:, :128], dec], axis=1)
                change = mm(left_side, rhs[unit])
                out_ref[0, rows, :] = (0.81 * m_ref[rows, :].astype(F32) + FACTOR * change).astype(BF16)

    def by_frequency(first, second):
        tiles = []
        for n in range(LOW // 2):
            one, two = first[8 * n:8 * n + 8], second[8 * n:8 * n + 8]
            tiles.append(jnp.where(top, one, pltpu.roll(two, 4, 0)))
            tiles.append(jnp.where(top, pltpu.roll(one, 4, 0), two))
        return tiles

    def picks_of(a, b):
        def mixed(ref, cols=slice(0, 128)):
            rows_a = pl.ds(pl.multiple_of(a * 8, 8), 8)
            rows_b = pl.ds(pl.multiple_of(b * 8, 8), 8)
            return jnp.where(top, ref[rows_a, cols], ref[rows_b, cols])

        return mixed(colmask), mixed(pull), [mixed(val, slice(k * 128, (k + 1) * 128)) for k in range(BAND)]

    def pack(stage, tiles, picks):
        mask, ahead, vals = picks
        thin = []
        for k in range(BAND):
            got = tiles[k]
            for f in range(k + 1, k + 9):
                got = jnp.where(vals[k] == f, tiles[f], got)
            moved = got
            for shift in range(1, 9):
                moved = jnp.where(ahead == shift, pltpu.roll(got, 128 - shift, 1), moved)
            thin.append(moved)
        for k in range(BAND // 2):
            packed = jnp.where(lane, thin[k], pltpu.roll(thin[k + BAND // 2], BAND, 1))
            send[stage, pl.ds(k, 8, stride=4), :] = packed

    def keep(unit, tiles, picks):
        mask, ahead, vals = picks
        for f in range(LOW):
            hit = jnp.zeros((8, 128), F32)
            for k in range(max(0, f - 8), min(7, f) + 1):
                hit = jnp.where(vals[k] == f, mask, hit)
            kept[unit, 8 * f:8 * f + 8, :] = hit * tiles[f]

    def own_base(owner, half):
        start = pl.multiple_of((owner % 2) * 128 + half * 64, 64)
        return gm[owner // 2, pl.ds(start, 64), :]

    def ship(stage, owner, i, column):
        return pltpu.make_async_remote_copy(
            src_ref=send.at[stage, pl.ds(i * 8, 8), :],
            dst_ref=recv.at[dp],
            send_sem=sum_send,
            recv_sem=sum_recv,
            device_id=(owner * Y + i, column),
            device_id_type=MESH,
        )

    def ship_own(stage, a, b):
        for i in range(Y):
            owner = a if i < Y // 2 else b

            @pl.when(owner * Y + i != dp)
            def _():
                ship(stage, owner, i, tensor).start()

            @pl.when(owner * Y + i == dp)
            def _():
                recv[dp] = send[stage, i * 8:(i + 1) * 8, :]

    def pair_step(s, carry):
        owners = owners_of(s)

        @pl.when(s > 0)
        def _():
            half_copy(owners[0][0], 0, mate).wait_recv()
            half_copy(owners[0][0], 0, mate).start()

            @pl.when(s == 1)
            def _():
                half_copy(left, 0, right).start()

            half_copy(owners[0][1], 1, mate).wait_recv()
            half_copy(owners[0][1], 1, mate).start()

            @pl.when(s == 1)
            def _():
                half_copy(right, 1, left).start()
                pl.semaphore_wait(y_token, Y - 1)
                pl.semaphore_signal(mate_token, inc=1, device_id=(dp, mate), device_id_type=MESH)
                for unit, (a, b) in enumerate(owners_of(0)):
                    ship_own(unit, a, b)

            write_pair(s - 1)

        half_copy(owners[1][0], 0, mate).wait_recv()
        half_copy(owners[1][1], 1, mate).wait_recv()

        quarters = [(a, 0) if half == 0 else (b, 1) for a, b in owners for half in range(2)]
        high, low = encode([xt[half_rows(owner, half), :] for owner, half in quarters])
        grid = mm(jnp.concatenate([high, low, high], axis=1), wx[:, 0:256])
        grid_a, grid_b = [], []
        for n, (owner, half) in enumerate(quarters):
            base = own_base(owner, half)
            grid_a.append(grid[n * 64:(n + 1) * 64, :128] + 0.81 * base)
            grid_b.append(grid[n * 64:(n + 1) * 64, 128:] + 0.9 * base)
        for unit, (a, b) in enumerate(owners):
            picks = picks_of(a, b)
            pack(s * 2 + unit, by_frequency(grid_b[2 * unit], grid_b[2 * unit + 1]), picks)
            keep(s * 2 + unit, by_frequency(grid_a[2 * unit], grid_a[2 * unit + 1]), picks)

        @pl.when(s > 0)
        def _():
            for unit, (a, b) in enumerate(owners):
                ship_own(s * 2 + unit, a, b)

        return carry

    lax.fori_loop(0, X - 1, pair_step, 0)

    pl.semaphore_wait(mate_token, 1)
    for copy in swaps:
        copy.wait_recv()
    for half in range(2):
        half_copy(far, half, mate).wait_recv()
        half_copy(far, half, mate).start()
    high, low = encode([xt[half_rows(far, half), :] for half in range(2)])
    triple = jnp.concatenate([high, low, high], axis=1)
    grid = mm(triple, wx[:, 128:384])
    bases = [own_base(far, half) for half in range(2)]
    picks = picks_of(far, far)
    pack(6, by_frequency(*[grid[n * 64:(n + 1) * 64, :128] + 0.9 * bases[n] for n in range(2)]), picks)
    ship_own(6, far, far)
    theirs = (mask_mate[...], pull_mate[...], [val_mate[:, k * 128:(k + 1) * 128] for k in range(BAND)])
    pack(8, by_frequency(*[grid[n * 64:(n + 1) * 64, 128:] + 0.9 * gm_mate[n * 64:(n + 1) * 64, :] for n in range(2)]), theirs)
    for i in range(Y):
        ship(8, far, i, mate).start()
    grid = mm(triple, wx[:, 0:128])
    keep(6, by_frequency(*[grid[n * 64:(n + 1) * 64] + 0.81 * bases[n] for n in range(2)]), picks)

    write_pair(X - 2)
    for half in range(2):
        half_copy(far_mate, half, mate).wait_recv()
    high, low = encode([xt[half_rows(far_mate, half), :] for half in range(2)])
    grid = mm(jnp.concatenate([high, low, high], axis=1), wx[:, 0:128])
    picks = picks_of(far_mate, far_mate)
    keep(7, by_frequency(*[grid[n * 64:(n + 1) * 64] + 0.81 * own_base(far_mate, n) for n in range(2)]), picks)
    write_pair(X - 1)

    for k in range(BAND):
        own[k] = val[pl.ds(pl.multiple_of(cz * 8, 8), 8), k * 128:(k + 1) * 128]
    own[BAND] = eight_of(push, cz)
    def wait_sums(count):
        some = recv.at[pl.ds(0, count)]
        pltpu.make_async_copy(some, some, sum_recv).wait()
        pltpu.make_async_copy(some, some, sum_send).wait()

    @pl.when(crossed)
    def _():
        wait_sums(GROUPS)

    @pl.when(jnp.logical_not(crossed))
    def _():
        wait_sums(GROUPS - 1)

    for copy in swaps:
        copy.wait_send()
    sent = xt.at[pl.ds(0, 7 * SHARD), :]
    pltpu.make_async_copy(sent, sent, gather_send).wait()


def finish(new_ref, recv, own, coldec, rowdec, out_hbm, upd_hbm, tot, upd, sem):
    cy = lax.axis_index("dp") % Y
    rows = ROWS // PARTS
    copies = [
        pltpu.make_async_copy(
            new_ref.at[0, pl.ds(n * rows, rows), :], out_hbm.at[0, pl.ds(n * rows, rows), :], sem.at[n]
        )
        for n in range(PARTS)
    ]
    for copy in copies:
        copy.start()
    tot[...] = jnp.zeros((32, 128), F32)
    tot[pl.ds(pl.multiple_of(cy * 8, 8), 8), :] = jnp.sum(recv[...], axis=0)
    behind = own[BAND]
    vals = [own[k] for k in range(BAND)]
    sums = []
    for part in range(2):
        for k in range(BAND // 2):
            packed = tot[pl.ds(k, 8, stride=4), :]
            if part:
                packed = pltpu.roll(packed, 128 - BAND, 1)
            full = jnp.zeros((8, 128), F32)
            for shift in range(9):
                moved = pltpu.roll(packed, shift, 1) if shift else packed
                full = jnp.where(behind == shift, moved, full)
            sums.append(full)
    kept = []
    for f in range(LOW):
        hit = jnp.zeros((8, 128), F32)
        for k in range(max(0, f - 8), min(7, f) + 1):
            hit = jnp.where(vals[k] == f, sums[k], hit)
        kept.append(hit)
    wide = widen(jnp.concatenate(kept, axis=0), coldec[...])
    high, low = split(wide)
    dec = rowdec[pl.ds(pl.multiple_of(cy * 128, 128), 128), :]
    upd[...] = mm(
        jnp.concatenate([dec[:, :128], dec], axis=1), jnp.concatenate([high, low, high], axis=0)
    )

    last = pltpu.make_async_copy(upd, upd_hbm, sem.at[PARTS])
    last.start()
    for copy in copies:
        copy.wait()
    last.wait()


def shards(inputs, out_grads, momentum, band):
    consts = [jnp.asarray(c) for c in constants()]
    band_t = jnp.transpose(band, (1, 2, 3, 0))
    hbm = pl.BlockSpec(memory_space=pltpu.HBM)
    vmem = pl.BlockSpec(memory_space=pltpu.VMEM)
    parts = pl.pallas_call(
        kernel,
        out_shape=(
            pltpu.VMEM(momentum.shape, BF16),
            pltpu.VMEM((GROUPS, 8, 128), F32),
            pltpu.VMEM((BAND + 1, 8, 128), F32),
            pltpu.VMEM((256, COLS), BF16),
            pltpu.VMEM((SHARD, 256), BF16),
        ),
        in_specs=[hbm] * 8,
        out_specs=(vmem,) * 5,
        scratch_shapes=[
            pltpu.VMEM((STEPS, TOK, SHARD), BF16),
            pltpu.VMEM((STEPS, TOK, COLS), BF16),
            pltpu.VMEM((ROWS, COLS), BF16),
            pltpu.VMEM((8, 2, 8, 64), jnp.int32),
            pltpu.VMEM((128, 256), F32),
            pltpu.VMEM((512, 256), F32),
            pltpu.VMEM((512, 256), F32),
            pltpu.VMEM((256, 512), F32),
            pltpu.VMEM((128, 256), BF16),
            pltpu.VMEM((512, 256), BF16),
            pltpu.VMEM((ROWS, STEPS * TOK), BF16),
            pltpu.VMEM((64, 2048), F32),
            pltpu.VMEM((64, 128), F32),
            pltpu.VMEM((64, 128), F32),
            pltpu.VMEM((64, 128), F32),
            pltpu.VMEM((768, 384), BF16),
            pltpu.VMEM((2, 768, COLS), BF16),
            pltpu.VMEM((X, 256, 128), F32),
            pltpu.VMEM((CHUNKS, 128, 128), F32),
            pltpu.VMEM((CHUNKS + 1, 32, 128), F32),
            pltpu.VMEM((128, 128), F32),
            pltpu.VMEM((8, 1024), F32),
            pltpu.VMEM((8, 128), F32),
            pltpu.VMEM((8, 128), F32),
            pltpu.SemaphoreType.DMA((8,)),
            pltpu.SemaphoreType.DMA((X,)),
            pltpu.SemaphoreType.DMA,
            pltpu.SemaphoreType.DMA((CHUNKS * 2,)),
            pltpu.SemaphoreType.DMA,
            pltpu.SemaphoreType.DMA,
            pltpu.SemaphoreType.DMA((5,)),
            pltpu.SemaphoreType.DMA((5,)),
            pltpu.SemaphoreType.REGULAR,
            pltpu.SemaphoreType.REGULAR,
            pltpu.SemaphoreType.REGULAR,
        ],
        compiler_params=pltpu.CompilerParams(
            collective_id=0, has_side_effects=True, vmem_limit_bytes=40 * 1024 * 1024
        ),
        name="demo_steps",
    )(*[pltpu.with_memory_space_constraint(a, pltpu.HBM) for a in (inputs, out_grads, momentum, band_t, *consts)])
    parts = [pltpu.with_memory_space_constraint(a, pltpu.VMEM) for a in parts]
    return pl.pallas_call(
        finish,
        out_shape=(pltpu.HBM(momentum.shape, BF16), pltpu.HBM((128, COLS), F32)),
        in_specs=[vmem] * 5,
        out_specs=(hbm, hbm),
        scratch_shapes=[
            pltpu.VMEM((32, 128), F32),
            pltpu.VMEM((128, COLS), F32),
            pltpu.SemaphoreType.DMA((PARTS + 1,)),
        ],
        compiler_params=pltpu.CompilerParams(vmem_limit_bytes=8 * 1024 * 1024),
        name="demo_finish",
    )(*parts)


def solution(mesh):
    return jax.shard_map(
        shards,
        mesh=mesh,
        in_specs=(
            P(None, "dp", "tensor"),
            P(None, "dp", "tensor"),
            P("dp", None, "tensor"),
            P(None, "tensor", None, None),
        ),
        out_specs=(P("dp", None, "tensor"), P("dp", "tensor")),
        check_vma=False,
    )
```

```python
import functools
import math

import jax
import jax.numpy as jnp
import ml_dtypes
import numpy as np
from jax import lax
from jax.experimental import pallas as pl
from jax.experimental.pallas import tpu as pltpu
from jax.sharding import PartitionSpec as P

MESH = pl.DeviceIdType.MESH
F32 = jnp.float32
BF16 = jnp.bfloat16
SPAN = 64
LOW = 16
BAND = 8
TOK = 128
ROWS = 4096
COLS = 512
SHARD = 512
STEPS = 2
X = 4
GROUPS = 32
Y = 4
Z = 8
HALF = SHARD // 2
CHUNKS = 8
PARTS = 1
FACTOR = 1.0 / math.sqrt(TOK)


def split_const(table):
    high = table.astype(ml_dtypes.bfloat16).astype(np.float32)
    return high, (table - high).astype(ml_dtypes.bfloat16).astype(np.float32)


def low_rows():
    freq = np.arange(LOW)[:, None]
    place = np.arange(SPAN)[None, :]
    table = np.sqrt(2.0 / SPAN) * np.cos(math.pi * (2.0 * place + 1.0) * freq / (2.0 * SPAN))
    table[0] /= math.sqrt(2.0)
    return table.astype(np.float32)


def constants():
    low = low_rows()
    four = np.zeros((LOW, 4, 4, SPAN), np.float32)
    enc = np.zeros((LOW, 8, 8, SPAN), np.float32)
    col = np.zeros((8, SPAN, 8, LOW), np.float32)
    for block in range(8):
        enc[:, block, block, :] = low
        col[block, :, block, :] = low.T
        if block < 4:
            four[:, block, block, :] = low
    rowenc = np.concatenate(split_const(four.reshape(64, 256)), axis=0)
    rowdec = np.concatenate(split_const(enc.reshape(128, 512).T), axis=1)
    colenc = np.concatenate(split_const(col.reshape(512, 128)), axis=1)
    high, lower = split_const(col.reshape(512, 128).T)
    zero = np.zeros((64, 256), np.float32)
    first = [high[:64, :256], lower[:64, :256], high[:64, :256], zero]
    second = [lower[64:, 256:], high[64:, 256:], zero, high[64:, 256:]]
    coldec = np.concatenate([np.concatenate(first, axis=0), np.concatenate(second, axis=0)], axis=1)
    return rowenc, rowdec, colenc, coldec


def split(a):
    high = a.astype(BF16)
    low = (a - high.astype(F32)).astype(BF16)
    return high, low


def mm(a, b):
    return jnp.dot(a, b, preferred_element_type=F32)


def widen(grids, coldec):
    lane = lax.broadcasted_iota(jnp.int32, grids.shape, 1) < 64
    turned = pltpu.roll(grids, 64, 1)
    high, low = split(grids)
    first = jnp.concatenate([jnp.where(lane, grids, turned).astype(BF16), low], axis=1)
    second = jnp.concatenate([jnp.where(lane, turned, grids).astype(BF16), low], axis=1)
    return jnp.concatenate([mm(first, coldec[:, :256]), mm(second, coldec[:, 256:])], axis=1)


def kernel(
    x_hbm, d_hbm, m_hbm, band_hbm, rowenc_hbm, rowdec_hbm, colenc_hbm, coldec_hbm,
    out_ref, recv, own, coldec, rowdec,
    xin, din, m_ref, band_ref, rowenc_in, rowdec_in, colenc_in, coldec_in, rowenc, colenc,
    xt, val, colmask, pull, push, wx, rhs, gm, kept, send, gm_mate, val_mate, pull_mate, mask_mate,
    load_sem, m_sem, gather_send, gather_recv, sum_send, sum_recv, swap_send, swap_recv,
    near_token, z_token, y_token, mate_token,
):
    dp = lax.axis_index("dp")
    tensor = lax.axis_index("tensor")
    cx = tensor // 2
    core = tensor % 2
    cz = dp // Y
    cy = dp % Y

    def tensor_of(hop, other):
        return 2 * ((cx + hop) % X) + (core + other) % 2

    mate = tensor_of(0, 1)
    right = tensor_of(1, 0)
    left = tensor_of(X - 1, 0)
    far = tensor_of(2, 0)
    far_mate = tensor_of(2, 1)
    crossed = cz == far_mate

    def load(src, dst, n):
        copy = pltpu.make_async_copy(src, dst, load_sem.at[n])
        copy.start()
        return copy

    x_loads = [
        load(x_hbm.at[:, :, half * 256:(half + 1) * 256], xin.at[:, :, half * 256:(half + 1) * 256], half)
        for half in range(2)
    ]
    def column(dz, dy):
        return (cz + dz) % Z * Y + (cy + dy) % Y

    z_far = [column(2, 0), column(Z - 2, 0)]
    y_peers = [column(0, n) for n in range(1, Y)]
    near = [(dp, mate), (dp, right), (dp, left)]
    beside = [column(1, 0), column(Z - 1, 0), column(0, 1), column(0, Y - 1)]
    near += [(peer, tensor) for peer in beside]
    barrier = pltpu.get_barrier_semaphore()
    for peer in near:
        pl.semaphore_signal(barrier, inc=1, device_id=peer, device_id_type=MESH)
    colenc_load = load(colenc_hbm, colenc_in, 2)
    d_load = load(d_hbm, din, 3)
    band_load = load(band_hbm, band_ref, 4)
    rowenc_load = load(rowenc_hbm, rowenc_in, 5)
    coldec_load = load(coldec_hbm, coldec_in, 6)
    rowdec_load = load(rowdec_hbm, rowdec_in, 7)

    def m_copy(p):
        rows = pl.ds(pl.multiple_of(p * 2 * SHARD, 2 * SHARD), 2 * SHARD)
        return pltpu.make_async_copy(m_hbm.at[0, rows, :], m_ref.at[rows, :], m_sem.at[p])

    for p in range(X):
        m_copy(p).start()

    def half_copy(owner, half, target):
        rows = pl.ds(pl.multiple_of(owner * SHARD + half * HALF, HALF), HALF)
        return pltpu.make_async_remote_copy(
            src_ref=xt.at[rows, :],
            dst_ref=xt.at[rows, :],
            send_sem=gather_send,
            recv_sem=gather_recv.at[owner * 2 + half],
            device_id=(dp, target),
            device_id_type=MESH,
        )

    def turn(half):
        x_loads[half].wait()
        rows = pl.ds(pl.multiple_of(tensor * SHARD + half * HALF, HALF), HALF)
        for step in range(STEPS):
            xt[rows, step * TOK:(step + 1) * TOK] = xin[step, :, half * HALF:(half + 1) * HALF].T

    turn(0)
    turn(1)
    pl.semaphore_wait(barrier, len(near))
    half_copy(tensor, 0, right).start()
    half_copy(tensor, 1, left).start()
    half_copy(tensor, 1, right).start()
    half_copy(tensor, 0, left).start()
    half_copy(tensor, 0, mate).start()
    half_copy(tensor, 1, mate).start()

    for peer in beside:
        pl.semaphore_signal(near_token, inc=1, device_id=(peer, tensor), device_id_type=MESH)

    colenc_load.wait()
    colenc[...] = colenc_in[...].astype(BF16)
    d_load.wait()
    both = mm(jnp.concatenate([din[0], din[1]], axis=0), colenc[...])
    hats = (both[:, :128] + both[:, 128:]) * FACTOR
    table = jnp.concatenate(
        [jnp.concatenate([0.9 * hats[:128], hats[:128]], axis=1), jnp.concatenate([hats[128:], hats[128:]], axis=1)],
        axis=0,
    )
    high, low = split(table)
    wx[0:256, 0:256] = high
    wx[256:512, 0:256] = high
    wx[512:768, 0:256] = low
    high, low = split(0.9 * din[0].astype(F32))
    for unit in range(2):
        rhs[unit, 0:128, :] = high
        rhs[unit, 128:256, :] = din[1]
        rhs[unit, 256:384, :] = low

    band_load.wait()
    picks = band_ref[...].reshape(128, 64).astype(F32).T.astype(BF16)
    away = lax.broadcasted_iota(jnp.int32, (128, 128), 0) - lax.broadcasted_iota(jnp.int32, (128, 128), 1) // LOW * 16
    for n in range(2 * BAND):
        val[:, n * 128:(n + 1) * 128] = mm(picks, (away == n).astype(F32).astype(BF16))
    place = (lax.broadcasted_iota(jnp.int32, (64, 128), 1) % LOW).astype(F32)
    seen = jnp.zeros((64, 128), F32)
    ahead = jnp.zeros((64, 128), F32)
    back = jnp.full((64, 128), -1.0, F32)
    for k in range(BAND):
        freq = val[:, (BAND + k) * 128:(BAND + k + 1) * 128]
        seen = jnp.where(freq == place, 1.0, seen)
        back = jnp.where(freq == place, place - k, back)
        ahead = jnp.where(place == k, freq - k, ahead)
    colmask[...] = seen
    pull[...] = ahead
    push[...] = back

    pl.semaphore_wait(near_token, len(beside))
    for peer in z_far:
        pl.semaphore_signal(z_token, inc=1, device_id=(peer, tensor), device_id_type=MESH)

    rowenc_load.wait()
    rowenc[...] = rowenc_in[...].astype(BF16)

    def encode(halves):
        wide = mm(rowenc[...], jnp.concatenate(halves, axis=1))
        wide = wide[:64] + wide[64:]
        size = halves[0].shape[1]
        return split(jnp.concatenate([wide[:, n * size:(n + 1) * size] for n in range(len(halves))], axis=0))

    def momentum_step(p, carry):
        m_copy(p).wait()
        high, low = encode(
            [m_ref[pl.ds(pl.multiple_of(p * 2 * SHARD + n * HALF, HALF), HALF), :] for n in range(4)]
        )
        both = mm(jnp.concatenate([high, low], axis=0), colenc[...])
        gm[p] = both[:256, :128] + both[:256, 128:] + both[256:, :128]
        return carry

    lax.fori_loop(0, X, momentum_step, 0)

    pl.semaphore_wait(z_token, 2)
    for peer in y_peers:
        pl.semaphore_signal(y_token, inc=1, device_id=(peer, tensor), device_id_type=MESH)

    def swap(src, dst, n):
        return pltpu.make_async_remote_copy(
            src_ref=src, dst_ref=dst, send_sem=swap_send.at[n], recv_sem=swap_recv.at[n],
            device_id=(dp, mate), device_id_type=MESH,
        )

    mate_rows = pl.ds(pl.multiple_of(far_mate * 8, 8), 8)
    swaps = [
        swap(wx.at[:, 128:256], wx.at[:, 256:384], 0),
        swap(gm.at[far_mate // 2, pl.ds(pl.multiple_of(far_mate % 2 * 128, 128), 128), :], gm_mate, 1),
        swap(val.at[mate_rows, 0:1024], val_mate, 2),
        swap(pull.at[mate_rows, :], pull_mate, 3),
        swap(colmask.at[mate_rows, :], mask_mate, 4),
    ]
    for copy in swaps:
        copy.start()
    coldec_load.wait()
    coldec[...] = coldec_in[...].astype(BF16)
    rowdec_load.wait()
    rowdec[...] = rowdec_in[...].astype(BF16)

    top = lax.broadcasted_iota(jnp.int32, (8, 128), 0) < 4
    lane = lax.broadcasted_iota(jnp.int32, (8, 128), 1) % LOW < BAND

    def eight_of(ref, owner):
        return ref[pl.ds(pl.multiple_of(owner * 8, 8), 8), :]

    def owners_of(s):
        hop_a = jnp.where(s == 0, 0, jnp.where(s == 1, X - 1, jnp.where(s == 2, 1, 2)))
        hop_b = jnp.where(s == 0, 0, jnp.where(s == 1, 1, jnp.where(s == 2, X - 1, 2)))
        return [(tensor_of(hop_a, other), tensor_of(hop_b, other)) for other in range(2)]

    def half_rows(owner, half):
        return pl.ds(pl.multiple_of(owner * SHARD + half * HALF, HALF), HALF)

    def write_pair(s):
        grids = jnp.concatenate([kept[s * 2], kept[s * 2 + 1]], axis=0)
        wide = widen(grids, coldec[...]) * (-1.0 / FACTOR)
        high, low = split(wide)
        for unit, (a, b) in enumerate(owners_of(s)):
            here = slice(unit * 128, (unit + 1) * 128)
            rhs[unit, 384:512, :] = high[here]
            rhs[unit, 512:640, :] = low[here]
            rhs[unit, 640:768, :] = high[here]
        for unit, (a, b) in enumerate(owners_of(s)):
            for half, owner in enumerate((a, b)):
                rows = half_rows(owner, half)
                part = xt[rows, :]
                dec = rowdec[half * HALF:(half + 1) * HALF, :]
                left_side = jnp.concatenate([part, part[:, :128], dec[:, :128], dec], axis=1)
                change = mm(left_side, rhs[unit])
                out_ref[0, rows, :] = (0.81 * m_ref[rows, :].astype(F32) + FACTOR * change).astype(BF16)

    def by_frequency(first, second):
        tiles = []
        for n in range(LOW // 2):
            one, two = first[8 * n:8 * n + 8], second[8 * n:8 * n + 8]
            tiles.append(jnp.where(top, one, pltpu.roll(two, 4, 0)))
            tiles.append(jnp.where(top, pltpu.roll(one, 4, 0), two))
        return tiles

    def picks_of(a, b):
        def mixed(ref, cols=slice(0, 128)):
            rows_a = pl.ds(pl.multiple_of(a * 8, 8), 8)
            rows_b = pl.ds(pl.multiple_of(b * 8, 8), 8)
            return jnp.where(top, ref[rows_a, cols], ref[rows_b, cols])

        return mixed(colmask), mixed(pull), [mixed(val, slice(k * 128, (k + 1) * 128)) for k in range(BAND)]

    def pack(stage, tiles, picks):
        mask, ahead, vals = picks
        thin = []
        for k in range(BAND):
            got = tiles[k]
            for f in range(k + 1, k + 9):
                got = jnp.where(vals[k] == f, tiles[f], got)
            moved = got
            for shift in range(1, 9):
                moved = jnp.where(ahead == shift, pltpu.roll(got, 128 - shift, 1), moved)
            thin.append(moved)
        for k in range(BAND // 2):
            packed = jnp.where(lane, thin[k], pltpu.roll(thin[k + BAND // 2], BAND, 1))
            send[stage, pl.ds(k, 8, stride=4), :] = packed

    def keep(unit, tiles, picks):
        mask, ahead, vals = picks
        for f in range(LOW):
            hit = jnp.zeros((8, 128), F32)
            for k in range(max(0, f - 8), min(7, f) + 1):
                hit = jnp.where(vals[k] == f, mask, hit)
            kept[unit, 8 * f:8 * f + 8, :] = hit * tiles[f]

    def own_base(owner, half):
        start = pl.multiple_of((owner % 2) * 128 + half * 64, 64)
        return gm[owner // 2, pl.ds(start, 64), :]

    def ship(stage, owner, i, column):
        return pltpu.make_async_remote_copy(
            src_ref=send.at[stage, pl.ds(i * 8, 8), :],
            dst_ref=recv.at[dp],
            send_sem=sum_send,
            recv_sem=sum_recv,
            device_id=(owner * Y + i, column),
            device_id_type=MESH,
        )

    def ship_own(stage, a, b):
        for i in range(Y):
            owner = a if i < Y // 2 else b

            @pl.when(owner * Y + i != dp)
            def _():
                ship(stage, owner, i, tensor).start()

            @pl.when(owner * Y + i == dp)
            def _():
                recv[dp] = send[stage, i * 8:(i + 1) * 8, :]

    def pair_step(s, carry):
        owners = owners_of(s)

        @pl.when(s > 0)
        def _():
            half_copy(owners[0][0], 0, mate).wait_recv()
            half_copy(owners[0][0], 0, mate).start()

            @pl.when(s == 1)
            def _():
                half_copy(left, 0, right).start()

            half_copy(owners[0][1], 1, mate).wait_recv()
            half_copy(owners[0][1], 1, mate).start()

            @pl.when(s == 1)
            def _():
                half_copy(right, 1, left).start()
                pl.semaphore_wait(y_token, Y - 1)
                pl.semaphore_signal(mate_token, inc=1, device_id=(dp, mate), device_id_type=MESH)
                for unit, (a, b) in enumerate(owners_of(0)):
                    ship_own(unit, a, b)

            write_pair(s - 1)

        half_copy(owners[1][0], 0, mate).wait_recv()
        half_copy(owners[1][1], 1, mate).wait_recv()

        quarters = [(a, 0) if half == 0 else (b, 1) for a, b in owners for half in range(2)]
        high, low = encode([xt[half_rows(owner, half), :] for owner, half in quarters])
        grid = mm(jnp.concatenate([high, low, high], axis=1), wx[:, 0:256])
        grid_a, grid_b = [], []
        for n, (owner, half) in enumerate(quarters):
            base = own_base(owner, half)
            grid_a.append(grid[n * 64:(n + 1) * 64, :128] + 0.81 * base)
            grid_b.append(grid[n * 64:(n + 1) * 64, 128:] + 0.9 * base)
        for unit, (a, b) in enumerate(owners):
            picks = picks_of(a, b)
            pack(s * 2 + unit, by_frequency(grid_b[2 * unit], grid_b[2 * unit + 1]), picks)
            keep(s * 2 + unit, by_frequency(grid_a[2 * unit], grid_a[2 * unit + 1]), picks)

        @pl.when(s > 0)
        def _():
            for unit, (a, b) in enumerate(owners):
                ship_own(s * 2 + unit, a, b)

        return carry

    lax.fori_loop(0, X - 1, pair_step, 0)

    pl.semaphore_wait(mate_token, 1)
    for copy in swaps:
        copy.wait_recv()
    for half in range(2):
        half_copy(far, half, mate).wait_recv()
        half_copy(far, half, mate).start()
    high, low = encode([xt[half_rows(far, half), :] for half in range(2)])
    triple = jnp.concatenate([high, low, high], axis=1)
    grid = mm(triple, wx[:, 128:384])
    bases = [own_base(far, half) for half in range(2)]
    picks = picks_of(far, far)
    pack(6, by_frequency(*[grid[n * 64:(n + 1) * 64, :128] + 0.9 * bases[n] for n in range(2)]), picks)
    ship_own(6, far, far)
    theirs = (mask_mate[...], pull_mate[...], [val_mate[:, k * 128:(k + 1) * 128] for k in range(BAND)])
    pack(8, by_frequency(*[grid[n * 64:(n + 1) * 64, 128:] + 0.9 * gm_mate[n * 64:(n + 1) * 64, :] for n in range(2)]), theirs)
    for i in range(Y):
        ship(8, far, i, mate).start()
    grid = mm(triple, wx[:, 0:128])
    keep(6, by_frequency(*[grid[n * 64:(n + 1) * 64] + 0.81 * bases[n] for n in range(2)]), picks)

    write_pair(X - 2)
    for half in range(2):
        half_copy(far_mate, half, mate).wait_recv()
    high, low = encode([xt[half_rows(far_mate, half), :] for half in range(2)])
    grid = mm(jnp.concatenate([high, low, high], axis=1), wx[:, 0:128])
    picks = picks_of(far_mate, far_mate)
    keep(7, by_frequency(*[grid[n * 64:(n + 1) * 64] + 0.81 * own_base(far_mate, n) for n in range(2)]), picks)
    write_pair(X - 1)

    for k in range(BAND):
        own[k] = val[pl.ds(pl.multiple_of(cz * 8, 8), 8), k * 128:(k + 1) * 128]
    own[BAND] = eight_of(push, cz)
    def wait_sums(count):
        some = recv.at[pl.ds(0, count)]
        pltpu.make_async_copy(some, some, sum_recv).wait()
        pltpu.make_async_copy(some, some, sum_send).wait()

    @pl.when(crossed)
    def _():
        wait_sums(GROUPS)

    @pl.when(jnp.logical_not(crossed))
    def _():
        wait_sums(GROUPS - 1)

    for copy in swaps:
        copy.wait_send()
    sent = xt.at[pl.ds(0, 7 * SHARD), :]
    pltpu.make_async_copy(sent, sent, gather_send).wait()


def finish(new_ref, recv, own, coldec, rowdec, out_hbm, upd_hbm, tot, upd, sem):
    cy = lax.axis_index("dp") % Y
    rows = ROWS // PARTS
    copies = [
        pltpu.make_async_copy(
            new_ref.at[0, pl.ds(n * rows, rows), :], out_hbm.at[0, pl.ds(n * rows, rows), :], sem.at[n]
        )
        for n in range(PARTS)
    ]
    for copy in copies:
        copy.start()
    tot[...] = jnp.zeros((32, 128), F32)
    tot[pl.ds(pl.multiple_of(cy * 8, 8), 8), :] = jnp.sum(recv[...], axis=0)
    behind = own[BAND]
    vals = [own[k] for k in range(BAND)]
    sums = []
    for part in range(2):
        for k in range(BAND // 2):
            packed = tot[pl.ds(k, 8, stride=4), :]
            if part:
                packed = pltpu.roll(packed, 128 - BAND, 1)
            full = jnp.zeros((8, 128), F32)
            for shift in range(9):
                moved = pltpu.roll(packed, shift, 1) if shift else packed
                full = jnp.where(behind == shift, moved, full)
            sums.append(full)
    kept = []
    for f in range(LOW):
        hit = jnp.zeros((8, 128), F32)
        for k in range(max(0, f - 8), min(7, f) + 1):
            hit = jnp.where(vals[k] == f, sums[k], hit)
        kept.append(hit)
    wide = widen(jnp.concatenate(kept, axis=0), coldec[...])
    high, low = split(wide)
    dec = rowdec[pl.ds(pl.multiple_of(cy * 128, 128), 128), :]
    upd[...] = mm(
        jnp.concatenate([dec[:, :128], dec], axis=1), jnp.concatenate([high, low, high], axis=0)
    )

    last = pltpu.make_async_copy(upd, upd_hbm, sem.at[PARTS])
    last.start()
    for copy in copies:
        copy.wait()
    last.wait()


def shards(inputs, out_grads, momentum, band):
    consts = [jnp.asarray(c) for c in constants()]
    band_t = jnp.transpose(band, (1, 2, 3, 0))
    hbm = pl.BlockSpec(memory_space=pltpu.HBM)
    vmem = pl.BlockSpec(memory_space=pltpu.VMEM)
    parts = pl.pallas_call(
        kernel,
        out_shape=(
            pltpu.VMEM(momentum.shape, BF16),
            pltpu.VMEM((GROUPS, 8, 128), F32),
            pltpu.VMEM((BAND + 1, 8, 128), F32),
            pltpu.VMEM((256, COLS), BF16),
            pltpu.VMEM((SHARD, 256), BF16),
        ),
        in_specs=[hbm] * 8,
        out_specs=(vmem,) * 5,
        scratch_shapes=[
            pltpu.VMEM((STEPS, TOK, SHARD), BF16),
            pltpu.VMEM((STEPS, TOK, COLS), BF16),
            pltpu.VMEM((ROWS, COLS), BF16),
            pltpu.VMEM((8, 2, 8, 64), jnp.int32),
            pltpu.VMEM((128, 256), F32),
            pltpu.VMEM((512, 256), F32),
            pltpu.VMEM((512, 256), F32),
            pltpu.VMEM((256, 512), F32),
            pltpu.VMEM((128, 256), BF16),
            pltpu.VMEM((512, 256), BF16),
            pltpu.VMEM((ROWS, STEPS * TOK), BF16),
            pltpu.VMEM((64, 2048), F32),
            pltpu.VMEM((64, 128), F32),
            pltpu.VMEM((64, 128), F32),
            pltpu.VMEM((64, 128), F32),
            pltpu.VMEM((768, 384), BF16),
            pltpu.VMEM((2, 768, COLS), BF16),
            pltpu.VMEM((X, 256, 128), F32),
            pltpu.VMEM((CHUNKS, 128, 128), F32),
            pltpu.VMEM((CHUNKS + 1, 32, 128), F32),
            pltpu.VMEM((128, 128), F32),
            pltpu.VMEM((8, 1024), F32),
            pltpu.VMEM((8, 128), F32),
            pltpu.VMEM((8, 128), F32),
            pltpu.SemaphoreType.DMA((8,)),
            pltpu.SemaphoreType.DMA((X,)),
            pltpu.SemaphoreType.DMA,
            pltpu.SemaphoreType.DMA((CHUNKS * 2,)),
            pltpu.SemaphoreType.DMA,
            pltpu.SemaphoreType.DMA,
            pltpu.SemaphoreType.DMA((5,)),
            pltpu.SemaphoreType.DMA((5,)),
            pltpu.SemaphoreType.REGULAR,
            pltpu.SemaphoreType.REGULAR,
            pltpu.SemaphoreType.REGULAR,
            pltpu.SemaphoreType.REGULAR,
        ],
        compiler_params=pltpu.CompilerParams(
            collective_id=0, has_side_effects=True, vmem_limit_bytes=40 * 1024 * 1024
        ),
        name="demo_steps",
    )(*[pltpu.with_memory_space_constraint(a, pltpu.HBM) for a in (inputs, out_grads, momentum, band_t, *consts)])
    parts = [pltpu.with_memory_space_constraint(a, pltpu.VMEM) for a in parts]
    return pl.pallas_call(
        finish,
        out_shape=(pltpu.HBM(momentum.shape, BF16), pltpu.HBM((128, COLS), F32)),
        in_specs=[vmem] * 5,
        out_specs=(hbm, hbm),
        scratch_shapes=[
            pltpu.VMEM((32, 128), F32),
            pltpu.VMEM((128, COLS), F32),
            pltpu.SemaphoreType.DMA((PARTS + 1,)),
        ],
        compiler_params=pltpu.CompilerParams(vmem_limit_bytes=8 * 1024 * 1024),
        name="demo_finish",
    )(*parts)


def solution(mesh):
    return jax.shard_map(
        shards,
        mesh=mesh,
        in_specs=(
            P(None, "dp", "tensor"),
            P(None, "dp", "tensor"),
            P("dp", None, "tensor"),
            P(None, "tensor", None, None),
        ),
        out_specs=(P("dp", None, "tensor"), P("dp", "tensor")),
        check_vma=False,
    )
```

```python
import functools
import math

import jax
import jax.numpy as jnp
import ml_dtypes
import numpy as np
from jax import lax
from jax.experimental import pallas as pl
from jax.experimental.pallas import tpu as pltpu
from jax.sharding import PartitionSpec as P

MESH = pl.DeviceIdType.MESH
F32 = jnp.float32
BF16 = jnp.bfloat16
SPAN = 64
LOW = 16
BAND = 8
TOK = 128
ROWS = 4096
COLS = 512
SHARD = 512
STEPS = 2
X = 4
GROUPS = 32
Y = 4
Z = 8
HALF = SHARD // 2
CHUNKS = 8
PARTS = 1
FACTOR = 1.0 / math.sqrt(TOK)


def split_const(table):
    high = table.astype(ml_dtypes.bfloat16).astype(np.float32)
    return high, (table - high).astype(ml_dtypes.bfloat16).astype(np.float32)


def low_rows():
    freq = np.arange(LOW)[:, None]
    place = np.arange(SPAN)[None, :]
    table = np.sqrt(2.0 / SPAN) * np.cos(math.pi * (2.0 * place + 1.0) * freq / (2.0 * SPAN))
    table[0] /= math.sqrt(2.0)
    return table.astype(np.float32)


def constants():
    low = low_rows()
    four = np.zeros((LOW, 4, 4, SPAN), np.float32)
    enc = np.zeros((LOW, 8, 8, SPAN), np.float32)
    col = np.zeros((8, SPAN, 8, LOW), np.float32)
    for block in range(8):
        enc[:, block, block, :] = low
        col[block, :, block, :] = low.T
        if block < 4:
            four[:, block, block, :] = low
    rowenc = np.concatenate(split_const(four.reshape(64, 256)), axis=0)
    rowdec = np.concatenate(split_const(enc.reshape(128, 512).T), axis=1)
    colenc = np.concatenate(split_const(col.reshape(512, 128)), axis=1)
    high, lower = split_const(col.reshape(512, 128).T)
    zero = np.zeros((64, 256), np.float32)
    first = [high[:64, :256], lower[:64, :256], high[:64, :256], zero]
    second = [lower[64:, 256:], high[64:, 256:], zero, high[64:, 256:]]
    coldec = np.concatenate([np.concatenate(first, axis=0), np.concatenate(second, axis=0)], axis=1)
    return rowenc, rowdec, colenc, coldec


def split(a):
    high = a.astype(BF16)
    low = (a - high.astype(F32)).astype(BF16)
    return high, low


def mm(a, b):
    return jnp.dot(a, b, preferred_element_type=F32)


def widen(grids, coldec):
    lane = lax.broadcasted_iota(jnp.int32, grids.shape, 1) < 64
    turned = pltpu.roll(grids, 64, 1)
    high, low = split(grids)
    first = jnp.concatenate([jnp.where(lane, grids, turned).astype(BF16), low], axis=1)
    second = jnp.concatenate([jnp.where(lane, turned, grids).astype(BF16), low], axis=1)
    return jnp.concatenate([mm(first, coldec[:, :256]), mm(second, coldec[:, 256:])], axis=1)


def kernel(
    x_hbm, d_hbm, m_hbm, band_hbm, rowenc_hbm, rowdec_hbm, colenc_hbm, coldec_hbm,
    out_ref, recv, own, coldec, rowdec,
    xin, din, m_ref, band_ref, rowenc_in, rowdec_in, colenc_in, coldec_in, rowenc, colenc,
    xt, val, colmask, pull, push, wx, rhs, gm, kept, send, gm_mate, val_mate, pull_mate, mask_mate,
    load_sem, m_sem, gather_send, gather_recv, sum_send, sum_recv, swap_send, swap_recv,
    near_token, z_token, y_token, mate_token,
):
    dp = lax.axis_index("dp")
    tensor = lax.axis_index("tensor")
    cx = tensor // 2
    core = tensor % 2
    cz = dp // Y
    cy = dp % Y

    def tensor_of(hop, other):
        return 2 * ((cx + hop) % X) + (core + other) % 2

    mate = tensor_of(0, 1)
    right = tensor_of(1, 0)
    left = tensor_of(X - 1, 0)
    far = tensor_of(2, 0)
    far_mate = tensor_of(2, 1)
    crossed = cz == far_mate

    def load(src, dst, n):
        copy = pltpu.make_async_copy(src, dst, load_sem.at[n])
        copy.start()
        return copy

    x_loads = [
        load(x_hbm.at[:, :, half * 256:(half + 1) * 256], xin.at[:, :, half * 256:(half + 1) * 256], half)
        for half in range(2)
    ]
    def column(dz, dy):
        return (cz + dz) % Z * Y + (cy + dy) % Y

    z_far = [column(2, 0), column(Z - 2, 0)]
    y_peers = [column(0, n) for n in range(1, Y)]
    near = [(dp, mate), (dp, right), (dp, left)]
    beside = [column(1, 0), column(Z - 1, 0), column(0, 1), column(0, Y - 1)]
    near += [(peer, tensor) for peer in beside]
    barrier = pltpu.get_barrier_semaphore()
    for peer in near:
        pl.semaphore_signal(barrier, inc=1, device_id=peer, device_id_type=MESH)
    colenc_load = load(colenc_hbm, colenc_in, 2)
    d_load = load(d_hbm, din, 3)
    band_load = load(band_hbm, band_ref, 4)
    rowenc_load = load(rowenc_hbm, rowenc_in, 5)
    coldec_load = load(coldec_hbm, coldec_in, 6)
    rowdec_load = load(rowdec_hbm, rowdec_in, 7)

    def m_copy(p):
        rows = pl.ds(pl.multiple_of(p * 2 * SHARD, 2 * SHARD), 2 * SHARD)
        return pltpu.make_async_copy(m_hbm.at[0, rows, :], m_ref.at[rows, :], m_sem.at[p])

    for p in range(X):
        m_copy(p).start()

    def half_copy(owner, half, target):
        rows = pl.ds(pl.multiple_of(owner * SHARD + half * HALF, HALF), HALF)
        return pltpu.make_async_remote_copy(
            src_ref=xt.at[rows, :],
            dst_ref=xt.at[rows, :],
            send_sem=gather_send,
            recv_sem=gather_recv.at[owner * 2 + half],
            device_id=(dp, target),
            device_id_type=MESH,
        )

    def turn(half):
        x_loads[half].wait()
        rows = pl.ds(pl.multiple_of(tensor * SHARD + half * HALF, HALF), HALF)
        for step in range(STEPS):
            xt[rows, step * TOK:(step + 1) * TOK] = xin[step, :, half * HALF:(half + 1) * HALF].T

    turn(0)
    turn(1)
    pl.semaphore_wait(barrier, len(near))
    half_copy(tensor, 0, right).start()
    half_copy(tensor, 1, left).start()
    half_copy(tensor, 1, right).start()
    half_copy(tensor, 0, left).start()
    half_copy(tensor, 0, mate).start()
    half_copy(tensor, 1, mate).start()

    for peer in beside:
        pl.semaphore_signal(near_token, inc=1, device_id=(peer, tensor), device_id_type=MESH)

    colenc_load.wait()
    colenc[...] = colenc_in[...].astype(BF16)
    d_load.wait()
    both = mm(jnp.concatenate([din[0], din[1]], axis=0), colenc[...])
    hats = (both[:, :128] + both[:, 128:]) * FACTOR
    table = jnp.concatenate(
        [jnp.concatenate([0.9 * hats[:128], hats[:128]], axis=1), jnp.concatenate([hats[128:], hats[128:]], axis=1)],
        axis=0,
    )
    high, low = split(table)
    wx[0:256, 0:256] = high
    wx[256:512, 0:256] = high
    wx[512:768, 0:256] = low
    high, low = split(0.9 * din[0].astype(F32))
    for unit in range(2):
        rhs[unit, 0:128, :] = high
        rhs[unit, 128:256, :] = din[1]
        rhs[unit, 256:384, :] = low

    band_load.wait()
    picks = band_ref[...].reshape(128, 64).astype(F32).T.astype(BF16)
    away = lax.broadcasted_iota(jnp.int32, (128, 128), 0) - lax.broadcasted_iota(jnp.int32, (128, 128), 1) // LOW * 16
    for n in range(2 * BAND):
        val[:, n * 128:(n + 1) * 128] = mm(picks, (away == n).astype(F32).astype(BF16))
    place = (lax.broadcasted_iota(jnp.int32, (64, 128), 1) % LOW).astype(F32)
    seen = jnp.zeros((64, 128), F32)
    ahead = jnp.zeros((64, 128), F32)
    back = jnp.full((64, 128), -1.0, F32)
    for k in range(BAND):
        freq = val[:, (BAND + k) * 128:(BAND + k + 1) * 128]
        seen = jnp.where(freq == place, 1.0, seen)
        back = jnp.where(freq == place, place - k, back)
        ahead = jnp.where(place == k, freq - k, ahead)
    colmask[...] = seen
    pull[...] = ahead
    push[...] = back

    pl.semaphore_wait(near_token, len(beside))
    for peer in z_far:
        pl.semaphore_signal(z_token, inc=1, device_id=(peer, tensor), device_id_type=MESH)

    rowenc_load.wait()
    rowenc[...] = rowenc_in[...].astype(BF16)

    def encode(halves):
        wide = mm(rowenc[...], jnp.concatenate(halves, axis=1))
        wide = wide[:64] + wide[64:]
        size = halves[0].shape[1]
        return split(jnp.concatenate([wide[:, n * size:(n + 1) * size] for n in range(len(halves))], axis=0))

    def momentum_step(p, carry):
        m_copy(p).wait()
        high, low = encode(
            [m_ref[pl.ds(pl.multiple_of(p * 2 * SHARD + n * HALF, HALF), HALF), :] for n in range(4)]
        )
        both = mm(jnp.concatenate([high, low], axis=0), colenc[...])
        gm[p] = both[:256, :128] + both[:256, 128:] + both[256:, :128]
        return carry

    lax.fori_loop(0, X, momentum_step, 0)

    pl.semaphore_wait(z_token, 2)
    for peer in y_peers:
        pl.semaphore_signal(y_token, inc=1, device_id=(peer, tensor), device_id_type=MESH)

    def swap(src, dst, n):
        return pltpu.make_async_remote_copy(
            src_ref=src, dst_ref=dst, send_sem=swap_send.at[n], recv_sem=swap_recv.at[n],
            device_id=(dp, mate), device_id_type=MESH,
        )

    mate_rows = pl.ds(pl.multiple_of(far_mate * 8, 8), 8)
    swaps = [
        swap(wx.at[:, 128:256], wx.at[:, 256:384], 0),
        swap(gm.at[far_mate // 2, pl.ds(pl.multiple_of(far_mate % 2 * 128, 128), 128), :], gm_mate, 1),
        swap(val.at[mate_rows, 0:1024], val_mate, 2),
        swap(pull.at[mate_rows, :], pull_mate, 3),
        swap(colmask.at[mate_rows, :], mask_mate, 4),
    ]
    for copy in swaps:
        copy.start()
    coldec_load.wait()
    coldec[...] = coldec_in[...].astype(BF16)
    rowdec_load.wait()
    rowdec[...] = rowdec_in[...].astype(BF16)

    top = lax.broadcasted_iota(jnp.int32, (8, 128), 0) < 4
    lane = lax.broadcasted_iota(jnp.int32, (8, 128), 1) % LOW < BAND

    def eight_of(ref, owner):
        return ref[pl.ds(pl.multiple_of(owner * 8, 8), 8), :]

    def owners_of(s):
        hop_a = jnp.where(s == 0, 0, jnp.where(s == 1, X - 1, jnp.where(s == 2, 1, 2)))
        hop_b = jnp.where(s == 0, 0, jnp.where(s == 1, 1, jnp.where(s == 2, X - 1, 2)))
        return [(tensor_of(hop_a, other), tensor_of(hop_b, other)) for other in range(2)]

    def half_rows(owner, half):
        return pl.ds(pl.multiple_of(owner * SHARD + half * HALF, HALF), HALF)

    def write_pair(s):
        grids = jnp.concatenate([kept[s * 2], kept[s * 2 + 1]], axis=0)
        wide = widen(grids, coldec[...]) * (-1.0 / FACTOR)
        high, low = split(wide)
        for unit, (a, b) in enumerate(owners_of(s)):
            here = slice(unit * 128, (unit + 1) * 128)
            rhs[unit, 384:512, :] = high[here]
            rhs[unit, 512:640, :] = low[here]
            rhs[unit, 640:768, :] = high[here]
        for unit, (a, b) in enumerate(owners_of(s)):
            for half, owner in enumerate((a, b)):
                rows = half_rows(owner, half)
                part = xt[rows, :]
                dec = rowdec[half * HALF:(half + 1) * HALF, :]
                left_side = jnp.concatenate([part, part[:, :128], dec[:, :128], dec], axis=1)
                change = mm(left_side, rhs[unit])
                out_ref[0, rows, :] = (0.81 * m_ref[rows, :].astype(F32) + FACTOR * change).astype(BF16)

    def by_frequency(first, second):
        tiles = []
        for n in range(LOW // 2):
            one, two = first[8 * n:8 * n + 8], second[8 * n:8 * n + 8]
            tiles.append(jnp.where(top, one, pltpu.roll(two, 4, 0)))
            tiles.append(jnp.where(top, pltpu.roll(one, 4, 0), two))
        return tiles

    def picks_of(a, b):
        def mixed(ref, cols=slice(0, 128)):
            rows_a = pl.ds(pl.multiple_of(a * 8, 8), 8)
            rows_b = pl.ds(pl.multiple_of(b * 8, 8), 8)
            return jnp.where(top, ref[rows_a, cols], ref[rows_b, cols])

        return mixed(colmask), mixed(pull), [mixed(val, slice(k * 128, (k + 1) * 128)) for k in range(BAND)]

    def pack(stage, tiles, picks):
        mask, ahead, vals = picks
        thin = []
        for k in range(BAND):
            got = tiles[k]
            for f in range(k + 1, k + 9):
                got = jnp.where(vals[k] == f, tiles[f], got)
            moved = got
            for shift in range(1, 9):
                moved = jnp.where(ahead == shift, pltpu.roll(got, 128 - shift, 1), moved)
            thin.append(moved)
        for k in range(BAND // 2):
            packed = jnp.where(lane, thin[k], pltpu.roll(thin[k + BAND // 2], BAND, 1))
            send[stage, pl.ds(k, 8, stride=4), :] = packed

    def keep(unit, tiles, picks):
        mask, ahead, vals = picks
        for f in range(LOW):
            hit = jnp.zeros((8, 128), F32)
            for k in range(max(0, f - 8), min(7, f) + 1):
                hit = jnp.where(vals[k] == f, mask, hit)
            kept[unit, 8 * f:8 * f + 8, :] = hit * tiles[f]

    def own_base(owner, half):
        start = pl.multiple_of((owner % 2) * 128 + half * 64, 64)
        return gm[owner // 2, pl.ds(start, 64), :]

    def ship(stage, owner, i, column):
        return pltpu.make_async_remote_copy(
            src_ref=send.at[stage, pl.ds(i * 8, 8), :],
            dst_ref=recv.at[dp],
            send_sem=sum_send,
            recv_sem=sum_recv,
            device_id=(owner * Y + i, column),
            device_id_type=MESH,
        )

    def ship_own(stage, a, b):
        for i in range(Y):
            owner = a if i < Y // 2 else b

            @pl.when(owner * Y + i != dp)
            def _():
                ship(stage, owner, i, tensor).start()

            @pl.when(owner * Y + i == dp)
            def _():
                recv[dp] = send[stage, i * 8:(i + 1) * 8, :]

    def pair_step(s, carry):
        owners = owners_of(s)

        @pl.when(s > 0)
        def _():
            half_copy(owners[0][0], 0, mate).wait_recv()

            @pl.when(s == 1)
            def _():
                half_copy(left, 0, right).start()

            half_copy(owners[0][0], 0, mate).start()
            half_copy(owners[0][1], 1, mate).wait_recv()

            @pl.when(s == 1)
            def _():
                half_copy(right, 1, left).start()

            half_copy(owners[0][1], 1, mate).start()

            @pl.when(s == 1)
            def _():
                pl.semaphore_wait(y_token, Y - 1)
                pl.semaphore_signal(mate_token, inc=1, device_id=(dp, mate), device_id_type=MESH)
                for unit, (a, b) in enumerate(owners_of(0)):
                    ship_own(unit, a, b)

            write_pair(s - 1)

        half_copy(owners[1][0], 0, mate).wait_recv()
        half_copy(owners[1][1], 1, mate).wait_recv()

        quarters = [(a, 0) if half == 0 else (b, 1) for a, b in owners for half in range(2)]
        high, low = encode([xt[half_rows(owner, half), :] for owner, half in quarters])
        grid = mm(jnp.concatenate([high, low, high], axis=1), wx[:, 0:256])
        grid_a, grid_b = [], []
        for n, (owner, half) in enumerate(quarters):
            base = own_base(owner, half)
            grid_a.append(grid[n * 64:(n + 1) * 64, :128] + 0.81 * base)
            grid_b.append(grid[n * 64:(n + 1) * 64, 128:] + 0.9 * base)
        for unit, (a, b) in enumerate(owners):
            picks = picks_of(a, b)
            pack(s * 2 + unit, by_frequency(grid_b[2 * unit], grid_b[2 * unit + 1]), picks)
            keep(s * 2 + unit, by_frequency(grid_a[2 * unit], grid_a[2 * unit + 1]), picks)

        @pl.when(s > 0)
        def _():
            for unit, (a, b) in enumerate(owners):
                ship_own(s * 2 + unit, a, b)

        return carry

    lax.fori_loop(0, X - 1, pair_step, 0)

    pl.semaphore_wait(mate_token, 1)
    for copy in swaps:
        copy.wait_recv()
    for half in range(2):
        half_copy(far, half, mate).wait_recv()
    high, low = encode([xt[half_rows(far, half), :] for half in range(2)])
    triple = jnp.concatenate([high, low, high], axis=1)
    grid = mm(triple, wx[:, 128:384])
    bases = [own_base(far, half) for half in range(2)]
    picks = picks_of(far, far)
    pack(6, by_frequency(*[grid[n * 64:(n + 1) * 64, :128] + 0.9 * bases[n] for n in range(2)]), picks)
    ship_own(6, far, far)
    theirs = (mask_mate[...], pull_mate[...], [val_mate[:, k * 128:(k + 1) * 128] for k in range(BAND)])
    pack(8, by_frequency(*[grid[n * 64:(n + 1) * 64, 128:] + 0.9 * gm_mate[n * 64:(n + 1) * 64, :] for n in range(2)]), theirs)
    for i in range(Y):
        ship(8, far, i, mate).start()
    for half in range(2):
        half_copy(far, half, mate).start()
    grid = mm(triple, wx[:, 0:128])
    keep(6, by_frequency(*[grid[n * 64:(n + 1) * 64] + 0.81 * bases[n] for n in range(2)]), picks)

    write_pair(X - 2)
    for half in range(2):
        half_copy(far_mate, half, mate).wait_recv()
    high, low = encode([xt[half_rows(far_mate, half), :] for half in range(2)])
    grid = mm(jnp.concatenate([high, low, high], axis=1), wx[:, 0:128])
    picks = picks_of(far_mate, far_mate)
    keep(7, by_frequency(*[grid[n * 64:(n + 1) * 64] + 0.81 * own_base(far_mate, n) for n in range(2)]), picks)
    write_pair(X - 1)

    for k in range(BAND):
        own[k] = val[pl.ds(pl.multiple_of(cz * 8, 8), 8), k * 128:(k + 1) * 128]
    own[BAND] = eight_of(push, cz)
    def wait_sums(count):
        some = recv.at[pl.ds(0, count)]
        pltpu.make_async_copy(some, some, sum_recv).wait()
        pltpu.make_async_copy(some, some, sum_send).wait()

    @pl.when(crossed)
    def _():
        wait_sums(GROUPS)

    @pl.when(jnp.logical_not(crossed))
    def _():
        wait_sums(GROUPS - 1)

    for copy in swaps:
        copy.wait_send()
    sent = xt.at[pl.ds(0, 7 * SHARD), :]
    pltpu.make_async_copy(sent, sent, gather_send).wait()


def finish(new_ref, recv, own, coldec, rowdec, out_hbm, upd_hbm, tot, upd, sem):
    cy = lax.axis_index("dp") % Y
    rows = ROWS // PARTS
    copies = [
        pltpu.make_async_copy(
            new_ref.at[0, pl.ds(n * rows, rows), :], out_hbm.at[0, pl.ds(n * rows, rows), :], sem.at[n]
        )
        for n in range(PARTS)
    ]
    for copy in copies:
        copy.start()
    tot[...] = jnp.zeros((32, 128), F32)
    tot[pl.ds(pl.multiple_of(cy * 8, 8), 8), :] = jnp.sum(recv[...], axis=0)
    behind = own[BAND]
    vals = [own[k] for k in range(BAND)]
    sums = []
    for part in range(2):
        for k in range(BAND // 2):
            packed = tot[pl.ds(k, 8, stride=4), :]
            if part:
                packed = pltpu.roll(packed, 128 - BAND, 1)
            full = jnp.zeros((8, 128), F32)
            for shift in range(9):
                moved = pltpu.roll(packed, shift, 1) if shift else packed
                full = jnp.where(behind == shift, moved, full)
            sums.append(full)
    kept = []
    for f in range(LOW):
        hit = jnp.zeros((8, 128), F32)
        for k in range(max(0, f - 8), min(7, f) + 1):
            hit = jnp.where(vals[k] == f, sums[k], hit)
        kept.append(hit)
    wide = widen(jnp.concatenate(kept, axis=0), coldec[...])
    high, low = split(wide)
    dec = rowdec[pl.ds(pl.multiple_of(cy * 128, 128), 128), :]
    upd[...] = mm(
        jnp.concatenate([dec[:, :128], dec], axis=1), jnp.concatenate([high, low, high], axis=0)
    )

    last = pltpu.make_async_copy(upd, upd_hbm, sem.at[PARTS])
    last.start()
    for copy in copies:
        copy.wait()
    last.wait()


def shards(inputs, out_grads, momentum, band):
    consts = [jnp.asarray(c) for c in constants()]
    band_t = jnp.transpose(band, (1, 2, 3, 0))
    hbm = pl.BlockSpec(memory_space=pltpu.HBM)
    vmem = pl.BlockSpec(memory_space=pltpu.VMEM)
    parts = pl.pallas_call(
        kernel,
        out_shape=(
            pltpu.VMEM(momentum.shape, BF16),
            pltpu.VMEM((GROUPS, 8, 128), F32),
            pltpu.VMEM((BAND + 1, 8, 128), F32),
            pltpu.VMEM((256, COLS), BF16),
            pltpu.VMEM((SHARD, 256), BF16),
        ),
        in_specs=[hbm] * 8,
        out_specs=(vmem,) * 5,
        scratch_shapes=[
            pltpu.VMEM((STEPS, TOK, SHARD), BF16),
            pltpu.VMEM((STEPS, TOK, COLS), BF16),
            pltpu.VMEM((ROWS, COLS), BF16),
            pltpu.VMEM((8, 2, 8, 64), jnp.int32),
            pltpu.VMEM((128, 256), F32),
            pltpu.VMEM((512, 256), F32),
            pltpu.VMEM((512, 256), F32),
            pltpu.VMEM((256, 512), F32),
            pltpu.VMEM((128, 256), BF16),
            pltpu.VMEM((512, 256), BF16),
            pltpu.VMEM((ROWS, STEPS * TOK), BF16),
            pltpu.VMEM((64, 2048), F32),
            pltpu.VMEM((64, 128), F32),
            pltpu.VMEM((64, 128), F32),
            pltpu.VMEM((64, 128), F32),
            pltpu.VMEM((768, 384), BF16),
            pltpu.VMEM((2, 768, COLS), BF16),
            pltpu.VMEM((X, 256, 128), F32),
            pltpu.VMEM((CHUNKS, 128, 128), F32),
            pltpu.VMEM((CHUNKS + 1, 32, 128), F32),
            pltpu.VMEM((128, 128), F32),
            pltpu.VMEM((8, 1024), F32),
            pltpu.VMEM((8, 128), F32),
            pltpu.VMEM((8, 128), F32),
            pltpu.SemaphoreType.DMA((8,)),
            pltpu.SemaphoreType.DMA((X,)),
            pltpu.SemaphoreType.DMA,
            pltpu.SemaphoreType.DMA((CHUNKS * 2,)),
            pltpu.SemaphoreType.DMA,
            pltpu.SemaphoreType.DMA,
            pltpu.SemaphoreType.DMA((5,)),
            pltpu.SemaphoreType.DMA((5,)),
            pltpu.SemaphoreType.REGULAR,
            pltpu.SemaphoreType.REGULAR,
            pltpu.SemaphoreType.REGULAR,
            pltpu.SemaphoreType.REGULAR,
        ],
        compiler_params=pltpu.CompilerParams(
            collective_id=0, has_side_effects=True, vmem_limit_bytes=40 * 1024 * 1024
        ),
        name="demo_steps",
    )(*[pltpu.with_memory_space_constraint(a, pltpu.HBM) for a in (inputs, out_grads, momentum, band_t, *consts)])
    parts = [pltpu.with_memory_space_constraint(a, pltpu.VMEM) for a in parts]
    return pl.pallas_call(
        finish,
        out_shape=(pltpu.HBM(momentum.shape, BF16), pltpu.HBM((128, COLS), F32)),
        in_specs=[vmem] * 5,
        out_specs=(hbm, hbm),
        scratch_shapes=[
            pltpu.VMEM((32, 128), F32),
            pltpu.VMEM((128, COLS), F32),
            pltpu.SemaphoreType.DMA((PARTS + 1,)),
        ],
        compiler_params=pltpu.CompilerParams(vmem_limit_bytes=8 * 1024 * 1024),
        name="demo_finish",
    )(*parts)


def solution(mesh):
    return jax.shard_map(
        shards,
        mesh=mesh,
        in_specs=(
            P(None, "dp", "tensor"),
            P(None, "dp", "tensor"),
            P("dp", None, "tensor"),
            P(None, "tensor", None, None),
        ),
        out_specs=(P("dp", None, "tensor"), P("dp", "tensor")),
        check_vma=False,
    )
```
